32 devices in a mesh: group: 2 (over x), space: 16 (over z, y, core).
Axes of the slice: x: 2, y: 2, z: 4, core: 2. Of those that a mesh axis runs over, the one named last changes fastest.
Arguments:
- source: float32 [128, 32768], P('space', 'group'), parts along dimension 1, may hold values from -6 to 6
- blocks: float32 [512, 64, 448], P(('group', 'space')), parts along dimension 0, as said below
- columns: int32 [512, 7], P(('group', 'space')), parts along dimension 0, may hold values from 0 to 23, as said below
- rows_up: int32 [128], P(('group', 'space')), parts along dimension 0, may hold values from 0 to 15, as said below
- rows_down: int32 [128], P(('group', 'space')), parts along dimension 0, may hold values from 0 to 15, as said below
Outputs:
- field: float32 [128, 32768], P('space', 'group'), parts along dimension 1
The draws below stay inside these ranges and needn't reach their ends.
There are 2 independent parts, one for each index of `group`. The reference program is written for one: setup_inputs(seed, part) draws one part's arguments, and reference() takes and returns one part's arrays. A program takes and returns all parts, laid end to end along the dimension named above; each array names one. Nothing has to cross between parts.
Inputs may be any that keep to these rules, and one draw needn't show every extreme that they name: `columns`: entry 0 of each row is the row itself, entry 1 a column from 16 to 19, entry 2 one from 20 on, entries 3 to 6 below 16; every received row is named by some row of its device. `rows_up`: 4 distinct row numbers of each device; device 0's include row 0 and row 15. `rows_down`: 4 distinct row numbers of each device; device 1's include row 0 and row 15. `blocks`: slot 0 holds a diagonal of 3 to 5 plus small entries; all other entries are small.
All inputs are finite; a program needn't handle non-finite values.
Results may differ from the reference program's by a relative error of at most 0.0003.
Values sent between devices are 32-bit elements; how exact they have to be, the bound alone decides.
No kernel may reach another device: no remote copies, remote signals or barrier semaphores. Data moves between devices by JAX's collectives and lax.ppermute only.
A program may use at most 64 MiB of HBM per device.

```python
import math
import jax
import jax.numpy as jnp
from jax import lax

BS = 64
SLOTS = 7
L = 128
HALO = 4
BR_DEV = 16
NROWS = 256
N_SPACE = 16


def draw_blocks(key, part):
    key = jax.random.fold_in(key, 11)
    noise_key, diag_key = jax.random.split(key)
    sigma = 0.75 / math.sqrt(7 * BS)
    noise = jax.random.normal(noise_key, (NROWS, BS, SLOTS * BS), jnp.float32) * sigma
    diagonal = jax.random.uniform(diag_key, (NROWS, BS), jnp.float32, 3.0, 5.0)
    inner = jnp.arange(BS, dtype=jnp.int32)
    across = jnp.arange(SLOTS * BS, dtype=jnp.int32)
    unit = (inner[:, None] == across[None, :]).astype(jnp.float32)
    return noise + unit[None, :, :] * diagonal[:, :, None]


def draw_columns(key, part):
    key = jax.random.fold_in(key, 12)
    low_key, high_key, rest_key = jax.random.split(key, 3)
    rows = jnp.arange(NROWS, dtype=jnp.int32)
    local = rows % BR_DEV
    device = rows // BR_DEV
    low_off = jax.random.randint(low_key, (N_SPACE,), 0, HALO)
    high_off = jax.random.randint(high_key, (N_SPACE,), 0, HALO)
    below = BR_DEV + (local + low_off[device]) % HALO
    above = BR_DEV + HALO + (local + high_off[device]) % HALO
    others = jax.random.randint(rest_key, (NROWS, SLOTS - 3), 0, BR_DEV)
    return jnp.concatenate([local[:, None], below[:, None], above[:, None], others], axis=1).astype(jnp.int32)


def pick_rows(key, owner):
    keys = jax.random.split(key, N_SPACE)
    chosen = jax.vmap(lambda single: jax.random.permutation(single, BR_DEV)[:HALO])(keys).astype(jnp.int32)
    first = jnp.concatenate([jnp.array([0, BR_DEV - 1], dtype=jnp.int32), jnp.arange(1, HALO - 1, dtype=jnp.int32)])
    chosen = chosen.at[owner].set(first)
    return chosen.reshape(N_SPACE * HALO).astype(jnp.int32)


def draw_rows_up(key, part):
    key = jax.random.fold_in(key, 13)
    return pick_rows(key, 0)


def draw_rows_down(key, part):
    key = jax.random.fold_in(key, 14)
    return pick_rows(key, 1)


def block_levels(key, dims, pieces, smallest, top_value):
    loudness = 1.0
    for position, blocks in pieces:
        steps = jax.random.uniform(jax.random.fold_in(jax.random.fold_in(key, 6), position), (blocks,), jnp.float32, smallest / len(pieces), top_value / len(pieces))
        loudness = loudness * jnp.repeat(jnp.exp(steps), dims[position] // blocks).reshape((-1,) + (1,) * (len(dims) - 1 - position))
    return loudness


def normal_values(own_key, shape, scale, reach, cuts=(), kind=jnp.bfloat16):
    drawn = jax.random.normal(own_key, shape, jnp.float32) * scale
    if len(cuts) > 0:
        drawn = block_levels(own_key, shape, cuts, -0.22, 0.18) * drawn
    return jnp.clip(drawn, min=-reach, max=reach).astype(kind)


def setup_inputs(seed: int = 0, part: int = 0) -> dict:
    seeds = jax.random.split(jax.random.key(seed), 6)
    own_keys = jax.random.split(jax.random.fold_in(seeds[5], part), 6)
    source = normal_values(own_keys[0], (L, NROWS * BS), 1.0, 6.0, ((0, 16),), jnp.float32)
    blocks = draw_blocks(jax.random.fold_in(jax.random.fold_in(seeds[5], part), 71), part)
    columns = draw_columns(jax.random.fold_in(jax.random.fold_in(seeds[5], part), 71), part)
    rows_up = draw_rows_up(jax.random.fold_in(jax.random.fold_in(seeds[5], part), 71), part)
    rows_down = draw_rows_down(jax.random.fold_in(jax.random.fold_in(seeds[5], part), 71), part)
    return dict(source=source, blocks=blocks, columns=columns, rows_up=rows_up, rows_down=rows_down)


shift_scale = 2.0
diag_center = 4.0


def angles():
    steps = jnp.arange(L, dtype=jnp.int32)
    phase = (steps[:, None] * steps[None, :]) % L
    return phase.astype(jnp.float32) * (2.0 * jnp.pi / L)


def factors():
    freq = jnp.arange(L, dtype=jnp.int32).astype(jnp.float32) * (2.0 * jnp.pi / L)
    shift_re = shift_scale * (1.0 - jnp.cos(freq))
    shift_im = shift_scale * jnp.sin(freq)
    denom = (diag_center + shift_re) ** 2 + shift_im ** 2
    return shift_re, shift_im, (diag_center + shift_re) / denom, -shift_im / denom


def complex_mul(factor_re, factor_im, values):
    val_re = values[..., :L]
    val_im = values[..., L:]
    return jnp.concatenate([factor_re * val_re - factor_im * val_im, factor_re * val_im + factor_im * val_re], axis=-1)


def reference(source, blocks, columns, rows_up, rows_down):
    hp = lax.Precision.HIGHEST
    table = angles()
    cosines = jnp.cos(table)
    sines = jnp.sin(table)
    forward = jnp.concatenate([cosines, -sines], axis=1)
    spectrum = jnp.einsum("tn,tc->nc", source, forward, precision=hp).reshape(NROWS, BS, 2 * L)
    shift_re, shift_im, step_re, step_im = factors()

    rows = jnp.arange(NROWS, dtype=jnp.int32)
    device = (rows // BR_DEV)[:, None]
    own = device * BR_DEV + columns
    low_dev = jnp.maximum(device - 1, 0)
    low_pos = low_dev * HALO + jnp.clip(columns - BR_DEV, 0, HALO - 1)
    low_row = low_dev * BR_DEV + rows_up[low_pos]
    high_dev = jnp.minimum(device + 1, N_SPACE - 1)
    high_pos = high_dev * HALO + jnp.clip(columns - BR_DEV - HALO, 0, HALO - 1)
    high_row = high_dev * BR_DEV + rows_down[high_pos]
    outside = jnp.int32(NROWS)
    lower_pick = jnp.where(device > 0, low_row, outside)
    upper_pick = jnp.where(device < N_SPACE - 1, high_row, outside)
    global_cols = jnp.where(columns < BR_DEV, own, jnp.where(columns < BR_DEV + HALO, lower_pick, upper_pick)).astype(jnp.int32)

    def operate(values):
        padded = jnp.concatenate([values, jnp.zeros((1, BS, 2 * L), jnp.float32)], axis=0)

        def one_device(index):
            start = (index * BR_DEV).astype(jnp.int32)
            picks = lax.dynamic_slice_in_dim(global_cols, start, BR_DEV, 0)
            local_blocks = lax.dynamic_slice_in_dim(blocks, start, BR_DEV, 0)
            gathered = padded[picks].reshape(BR_DEV, SLOTS * BS, 2 * L)
            return jnp.einsum("rak,rkc->rac", local_blocks, gathered, precision=hp)

        applied = lax.map(one_device, jnp.arange(N_SPACE, dtype=jnp.int32)).reshape(NROWS, BS, 2 * L)
        return applied + complex_mul(shift_re, shift_im, values)

    iterate = complex_mul(step_re, step_im, spectrum)
    for sweep in range(3):
        iterate = iterate + complex_mul(step_re, step_im, spectrum - operate(iterate))
    inverse = jnp.concatenate([cosines, -sines], axis=1) / L
    return jnp.einsum("nc,tc->tn", iterate.reshape(NROWS * BS, 2 * L), inverse, precision=hp)
```

```python
import functools

import jax
import jax.numpy as jnp
import numpy as np
from jax import lax
from jax.experimental import pallas as pl
from jax.experimental.pallas import tpu as pltpu
from jax.sharding import PartitionSpec as P

BS = 64
SLOTS = 7
SHIFT_SCALE = 2.0
DIAG_CENTER = 4.0
LANES = 128
TERMS = 4
VMEM = pl.BlockSpec(memory_space=pltpu.VMEM)
SMEM = pl.BlockSpec(memory_space=pltpu.SMEM)


def time_filters(length):
    phase = np.exp(-2j * np.pi * np.arange(length) / length)
    step = 1.0 / (DIAG_CENTER + SHIFT_SCALE * (1.0 - phase))
    apart = np.arange(length)[:, None] - np.arange(length)[None, :]
    return [np.fft.ifft(step ** (m + 1)).real[apart % length] for m in range(TERMS)]


def halves(value):
    high = value.astype(jnp.bfloat16)
    return high, (value - high.astype(jnp.float32)).astype(jnp.bfloat16)


def mm(left, right):
    return jnp.dot(left, right, preferred_element_type=jnp.float32)


def mm_split(left, right_high, right_low):
    rows = left.shape[0]
    high, low = halves(left)
    both = mm(jnp.concatenate([high, low], axis=0), right_high)
    return both[:rows] + both[rows:] + mm(high, right_low)


def filter_mm(table, value):
    rows = table.shape[0] // 2
    high, low = halves(value)
    both = mm(table, high)
    return both[:rows] + both[rows:] + mm(table[:rows], low)


def build_kernel(count, me_ref, columns_ref, blocks_ref, high_ref, low_ref, full_ref):
    rows, size, _ = blocks_ref.shape
    halo = (full_ref.shape[0] // size - rows) // 2
    me = me_ref[0]
    even = lax.rem(me, 2) == 0
    full_ref[...] = jnp.zeros_like(full_ref)
    lane = lax.broadcasted_iota(jnp.int32, (size, 2 * size), 1)
    inner = lax.broadcasted_iota(jnp.int32, (size, 2 * size), 0)
    for pair in range(rows // 2):
        lanes = slice(pair * 2 * size, (pair + 1) * 2 * size)
        across = blocks_ref[2 * pair : 2 * pair + 2].reshape(2 * size, SLOTS * size).T
        for slot in range(SLOTS):
            piece = -across[slot * size : (slot + 1) * size]
            if slot == 0:
                piece = piece + jnp.where(lax.rem(lane, size) == inner, DIAG_CENTER, 0.0)
            for half in range(2):
                column = columns_ref[2 * pair + half, slot]
                kept = jnp.where(lane // size == half, piece, 0.0)
                if slot == 1:
                    column = jnp.where(even, column + halo, column)
                    kept = jnp.where(me == 0, 0.0, kept)
                if slot == 2:
                    column = jnp.where(even, column - halo, column)
                    kept = jnp.where(me == count - 1, 0.0, kept)
                at = pl.ds(pl.multiple_of(column * size, size), size)
                full_ref[at, lanes] += kept
    for start in range(0, full_ref.shape[0], size):
        high, low = halves(full_ref[start : start + size])
        high_ref[start : start + size] = high
        low_ref[start : start + size] = low


def pick(value_ref, rows_ref, out_ref):
    times, size = value_ref.shape[0], BS
    lane = lax.broadcasted_iota(jnp.int32, (times, 2 * size), 1)
    for pair in range(rows_ref.shape[0] // 2):
        parts = []
        for half in range(2):
            row = rows_ref[2 * pair + half]
            at = pl.ds(pl.multiple_of((row // 2) * 2 * size, 2 * size), 2 * size)
            tile = value_ref[:, at]
            parts.append(jnp.where(lax.rem(row, 2) == half, tile, pltpu.roll(tile, size, 1)))
        out_ref[:, pair * 2 * size : (pair + 1) * 2 * size] = jnp.where(lane < size, parts[0], parts[1])


def pick_both(me_ref, up_ref, down_ref, value_ref, inner_ref, outer_ref):
    even = lax.rem(me_ref[0], 2) == 0

    @pl.when(even)
    def _():
        pick(value_ref, up_ref, inner_ref)
        pick(value_ref, down_ref, outer_ref)

    @pl.when(jnp.logical_not(even))
    def _():
        pick(value_ref, down_ref, inner_ref)
        pick(value_ref, up_ref, outer_ref)


def first_kernel(me_ref, up_ref, down_ref, value_ref, inner_ref, outer_ref):
    pick_both(me_ref, up_ref, down_ref, value_ref, inner_ref, outer_ref)


def own_kernel(value_ref, high_ref, low_ref, out_ref):
    own = value_ref.shape[1]
    out_ref[...] = mm_split(value_ref[...], high_ref[:own], low_ref[:own])


def halo_product(inner_ref, outer_ref, high_ref, low_ref):
    both = jnp.concatenate([inner_ref[...], outer_ref[...]], axis=1)
    own = high_ref.shape[0] - both.shape[1]
    return mm_split(both, high_ref[own:], low_ref[own:])


def halo_kernel(me_ref, up_ref, down_ref, part_ref, from_inner, from_outer, high_ref, low_ref, out_ref, inner_ref, outer_ref):
    out_ref[...] = part_ref[...] + halo_product(from_inner, from_outer, high_ref, low_ref)
    pick_both(me_ref, up_ref, down_ref, out_ref, inner_ref, outer_ref)


def halo_last_kernel(me_ref, up_ref, down_ref, part_ref, from_inner, from_outer, high_ref, low_ref, table_ref, out_ref, inner_ref, outer_ref):
    value = part_ref[...] + halo_product(from_inner, from_outer, high_ref, low_ref)
    out_ref[...] = value
    pick_both(me_ref, up_ref, down_ref, out_ref, inner_ref, outer_ref)
    inner_ref[...] = filter_mm(table_ref[...], inner_ref[...])
    outer_ref[...] = filter_mm(table_ref[...], outer_ref[...])


def second_own_kernel(value_ref, start_ref, high_ref, low_ref, table0_ref, table1_ref, out_ref, total_ref):
    own_kernel(value_ref, high_ref, low_ref, out_ref)
    total_ref[...] = filter_mm(table0_ref[...], start_ref[...]) + filter_mm(table1_ref[...], value_ref[...])


def third_own_kernel(value_ref, total_ref, high_ref, low_ref, table2_ref, table3_ref, out_ref):
    own = value_ref.shape[1]
    value = value_ref[...]
    filtered = filter_mm(table3_ref[...], value)
    out_ref[...] = (
        total_ref[...] + filter_mm(table2_ref[...], value) + mm_split(filtered, high_ref[:own], low_ref[:own])
    )


def close_kernel(part_ref, from_inner, from_outer, high_ref, low_ref, out_ref):
    out_ref[...] = part_ref[...] + halo_product(from_inner, from_outer, high_ref, low_ref)


def call(kernel, outs, name, scratch=(), flops=1 << 28, specs=None):
    return pl.pallas_call(
        kernel,
        out_shape=outs,
        in_specs=specs,
        out_specs=jax.tree.map(lambda _: VMEM, outs),
        scratch_shapes=scratch,
        name=name,
        compiler_params=pltpu.CompilerParams(vmem_limit_bytes=32 << 20),
        cost_estimate=pl.CostEstimate(flops=flops, bytes_accessed=4 << 20, transcendentals=0),
    )


def per_device(source, blocks, columns, rows_up, rows_down):
    count = lax.axis_size("space")
    rows, halo = blocks.shape[0], rows_up.shape[0]
    own, width = rows * BS, halo * BS
    times = source.shape[0] * count
    me = lax.axis_index("space").reshape(1)
    f32 = lambda *shape: jax.ShapeDtypeStruct(shape, jnp.float32)
    bf16 = lambda *shape: jax.ShapeDtypeStruct(shape, jnp.bfloat16)
    tables = [
        jnp.concatenate(halves(jnp.asarray(table, jnp.float32)), axis=0) for table in time_filters(times)
    ]
    inner_pairs = [(i, i ^ 1) for i in range(count)]
    outer_pairs = [pair for i in range(1, count - 1, 2) for pair in ((i, i + 1), (i + 1, i))]

    def swap(inner, outer):
        return lax.ppermute(inner, "space", inner_pairs), lax.ppermute(outer, "space", outer_pairs)

    start = lax.all_to_all(source, "space", split_axis=1, concat_axis=0, tiled=True)
    high, low = call(
        functools.partial(build_kernel, count),
        (bf16(own + 2 * width, own), bf16(own + 2 * width, own)),
        "operator",
        scratch=[pltpu.VMEM((own + 2 * width, own), jnp.float32)],
        specs=[SMEM, SMEM, VMEM],
    )(me, columns, blocks)
    lists = (me, rows_up, rows_down)
    sent = (f32(times, width), f32(times, width))
    value = f32(times, own)

    inner, outer = call(first_kernel, sent, "first_rows", specs=[SMEM] * 3 + [VMEM])(*lists, start)
    inner, outer = swap(inner, outer)
    part = call(own_kernel, value, "own_1", specs=[VMEM] * 3)(start, high, low)
    once, inner, outer = call(halo_kernel, (value, *sent), "halo_1", specs=[SMEM] * 3 + [VMEM] * 5)(
        *lists, part, inner, outer, high, low
    )
    inner, outer = swap(inner, outer)
    part, total = call(second_own_kernel, (value, value), "own_2", specs=[VMEM] * 6)(
        once, start, high, low, tables[0], tables[1]
    )
    twice, inner, outer = call(halo_last_kernel, (value, *sent), "halo_2", specs=[SMEM] * 3 + [VMEM] * 6)(
        *lists, part, inner, outer, high, low, tables[3]
    )
    inner, outer = swap(inner, outer)
    part = call(third_own_kernel, value, "own_3", specs=[VMEM] * 6)(twice, total, high, low, tables[2], tables[3])
    timed = call(close_kernel, value, "halo_3", specs=[VMEM] * 5)(part, inner, outer, high, low)
    return lax.all_to_all(timed, "space", split_axis=0, concat_axis=1, tiled=True)


def solution(mesh):
    placed = (
        P("space", "group"),
        P(("group", "space"), None, None),
        P(("group", "space"), None),
        P(("group", "space")),
        P(("group", "space")),
    )
    return jax.shard_map(
        per_device, mesh=mesh, in_specs=placed, out_specs=P("space", "group"), check_vma=False
    )
```

```python
import functools

import jax
import jax.numpy as jnp
import numpy as np
from jax import lax
from jax.experimental import pallas as pl
from jax.experimental.pallas import tpu as pltpu
from jax.sharding import PartitionSpec as P

BS = 64
SLOTS = 7
SHIFT_SCALE = 2.0
DIAG_CENTER = 4.0
TERMS = 4
VMEM = pl.BlockSpec(memory_space=pltpu.VMEM)
SMEM = pl.BlockSpec(memory_space=pltpu.SMEM)
ANY = pl.BlockSpec(memory_space=pl.ANY)


def time_filters(length):
    phase = np.exp(-2j * np.pi * np.arange(length) / length)
    step = 1.0 / (DIAG_CENTER + SHIFT_SCALE * (1.0 - phase))
    apart = np.arange(length)[:, None] - np.arange(length)[None, :]
    return [np.fft.ifft(step ** (m + 1)).real[apart % length] for m in range(TERMS)]


def halves(value):
    high = value.astype(jnp.bfloat16)
    return high, (value - high.astype(jnp.float32)).astype(jnp.bfloat16)


def mm(left, right):
    return jnp.dot(left, right, preferred_element_type=jnp.float32)


def mm_split(left, right_high, right_low):
    rows = left.shape[0]
    high, low = halves(left)
    both = mm(jnp.concatenate([high, low], axis=0), right_high)
    return both[:rows] + both[rows:] + mm(high, right_low)


def filter_mm(table, value):
    rows = table.shape[0] // 2
    high, low = halves(value)
    both = mm(table, high)
    return both[:rows] + both[rows:] + mm(table[:rows], low)


def chosen(even, up_ref, down_ref, index, halo):
    first = jnp.where(even, up_ref[index % halo], down_ref[index % halo])
    second = jnp.where(even, down_ref[index % halo], up_ref[index % halo])
    return first if index < halo else second


def build_kernel(
    count, me_ref, columns_ref, up_ref, down_ref, blocks_in,
    high_ref, low_ref, sent_high_ref, sent_low_ref, place_ref, table_ref, blocks_ref, block_sems,
):
    rows, size, _ = blocks_ref.shape
    halo = up_ref.shape[0]
    pieces = [
        pltpu.make_async_copy(
            blocks_in.at[pl.ds(2 * pair, 2)], blocks_ref.at[pl.ds(2 * pair, 2)], block_sems.at[pair]
        )
        for pair in range(rows // 2)
    ]
    for copy in pieces:
        copy.start()
    me = me_ref[0]
    even = lax.rem(me, 2) == 0
    sent = [chosen(even, up_ref, down_ref, index, halo) for index in range(2 * halo)]
    for index in range(2 * halo):
        table_ref[SLOTS, index] = sent[index]
    for row in range(rows):
        for slot in range(SLOTS):
            column = columns_ref[slot, row]
            if slot in (1, 2):
                column = jnp.where(even, column + (halo if slot == 1 else -halo), column)
            table_ref[slot, row] = column
    lane = lax.broadcasted_iota(jnp.int32, (size, 2 * size), 1)
    inner = lax.broadcasted_iota(jnp.int32, (size, 2 * size), 0)
    for pair in range(rows // 2):
        pieces[pair].wait()
        lanes = slice(pair * 2 * size, (pair + 1) * 2 * size)
        across = -blocks_ref[2 * pair : 2 * pair + 2].reshape(2 * size, SLOTS * size).T
        part = [across[slot * size : (slot + 1) * size] for slot in range(SLOTS)]
        part[0] = part[0] + jnp.where(lax.rem(lane, size) == inner, DIAG_CENTER, 0.0)
        part[1] = jnp.where(me == 0, 0.0, part[1])
        part[2] = jnp.where(me == count - 1, 0.0, part[2])
        for later in range(3, SLOTS):
            for sooner in (0, *range(3, later)):
                same = [columns_ref[later, 2 * pair + half] == columns_ref[sooner, 2 * pair + half] for half in range(2)]
                moved = jnp.where(lane < size, same[0].astype(jnp.int32), same[1].astype(jnp.int32)) > 0
                part[sooner] = part[sooner] + jnp.where(moved, part[later], 0.0)
                part[later] = jnp.where(moved, 0.0, part[later])
        for slot in range(SLOTS):
            high, low = halves(part[slot])
            high_ref[slot * size : (slot + 1) * size, lanes] = high
            low_ref[slot * size : (slot + 1) * size, lanes] = low
    wide = lax.broadcasted_iota(jnp.int32, (2 * size, 2 * size), 1)
    for pair in range(halo):
        lanes = slice(pair * 2 * size, (pair + 1) * 2 * size)
        for whole_ref, few_ref in ((high_ref, sent_high_ref), (low_ref, sent_low_ref)):
            parts = []
            for half in range(2):
                row = sent[2 * pair + half]
                at = pl.ds(pl.multiple_of((row // 2) * 2 * size, 2 * size), 2 * size)
                tile = whole_ref[size : 3 * size, at].astype(jnp.float32)
                parts.append(jnp.where(lax.rem(row, 2) == half, tile, pltpu.roll(tile, size, 1)))
            few_ref[:, lanes] = jnp.where(wide < size, parts[0], parts[1]).astype(jnp.bfloat16)
        across = lax.broadcasted_iota(jnp.int32, (place_ref.shape[0], 2 * size), 1)
        place_ref[:, lanes] = jnp.where(across < size, sent[2 * pair], sent[2 * pair + 1] - 1) * size + across


def store_sent(value, inner_ref, outer_ref):
    width = inner_ref.shape[1]
    inner_ref[...] = value[:, :width]
    outer_ref[...] = value[:, width:]


def picked(value, pick_ref):
    high, low = halves(value)
    rows = high.shape[0]
    both = mm(jnp.concatenate([high, low], axis=0), pick_ref[...])
    return both[:rows] + both[rows:]


def first_kernel(value_ref, place_ref, inner_ref, outer_ref, pick_ref):
    down = lax.broadcasted_iota(jnp.int32, pick_ref.shape, 0)
    pick_ref[...] = jnp.where(down == place_ref[0:1, :], 1.0, 0.0).astype(jnp.bfloat16)
    store_sent(picked(value_ref[...], pick_ref), inner_ref, outer_ref)


def own_first_kernel(
    value_ref, blocks_high, blocks_low, sent_high, sent_low, pick_ref, table_in,
    out_ref, sent_ref, high_ref, low_ref, halo_high, halo_low, table_ref, sem,
):
    times, own = value_ref.shape
    size = BS
    rows = own // size
    copy = pltpu.make_async_copy(table_in, table_ref, sem)
    copy.start()
    for ref in (high_ref, low_ref, halo_high, halo_low):
        ref[...] = jnp.zeros_like(ref)
    copy.wait()
    for slot in reversed(range(SLOTS)):
        for row in range(rows):
            at = pl.ds(pl.multiple_of(table_ref[slot, row] * size, size), size)
            lanes = slice(row * size, (row + 1) * size)
            high_ref[at, lanes] = blocks_high[slot * size : (slot + 1) * size, lanes]
            low_ref[at, lanes] = blocks_low[slot * size : (slot + 1) * size, lanes]
    for index in range(sent_high.shape[1] // size):
        row = table_ref[SLOTS, index]
        lanes = slice(index * size, (index + 1) * size)
        for slot in (1, 2):
            at = pl.ds(pl.multiple_of((table_ref[slot, row] - rows) * size, size), size)
            halo_high[at, lanes] = sent_high[(slot - 1) * size : slot * size, lanes]
            halo_low[at, lanes] = sent_low[(slot - 1) * size : slot * size, lanes]
    out_ref[...] = mm_split(value_ref[...], high_ref[:own], low_ref[:own])
    sent_ref[...] = picked(out_ref[...], pick_ref)


def halo_product(inner_ref, outer_ref, high, low):
    both = jnp.concatenate([inner_ref[...], outer_ref[...]], axis=1)
    return mm_split(both, high, low)


def send_kernel(part_ref, from_inner, from_outer, halo_high, halo_low, inner_ref, outer_ref):
    value = part_ref[...] + halo_product(from_inner, from_outer, halo_high[...], halo_low[...])
    store_sent(value, inner_ref, outer_ref)


def send_last_kernel(part_ref, from_inner, from_outer, halo_high, halo_low, table_ref, inner_ref, outer_ref):
    value = part_ref[...] + halo_product(from_inner, from_outer, halo_high[...], halo_low[...])
    store_sent(filter_mm(table_ref[...], value), inner_ref, outer_ref)


def own_second_kernel(
    start_ref, part_ref, from_inner, from_outer, high_ref, low_ref, pick_ref, table0_ref, table1_ref,
    out_ref, sent_ref, total_ref,
):
    own = part_ref.shape[1]
    value = part_ref[...] + halo_product(from_inner, from_outer, high_ref[own:], low_ref[own:])
    out_ref[...] = mm_split(value, high_ref[:own], low_ref[:own])
    sent_ref[...] = picked(out_ref[...], pick_ref)
    total_ref[...] = filter_mm(table0_ref[...], start_ref[...]) + filter_mm(table1_ref[...], value)


def own_third_kernel(part_ref, from_inner, from_outer, total_ref, high_ref, low_ref, table2_ref, table3_ref, out_ref):
    own = part_ref.shape[1]
    value = part_ref[...] + halo_product(from_inner, from_outer, high_ref[own:], low_ref[own:])
    filtered = filter_mm(table3_ref[...], value)
    out_ref[...] = (
        total_ref[...] + filter_mm(table2_ref[...], value) + mm_split(filtered, high_ref[:own], low_ref[:own])
    )


def close_kernel(part_ref, from_inner, from_outer, high_ref, low_ref, out_ref):
    own = part_ref.shape[1]
    out_ref[...] = part_ref[...] + halo_product(from_inner, from_outer, high_ref[own:], low_ref[own:])


def call(kernel, outs, name, ins, out_specs=None, scratch=(), moved=4 << 20):
    return pl.pallas_call(
        kernel,
        out_shape=outs,
        in_specs=ins,
        out_specs=jax.tree.map(lambda _: VMEM, outs) if out_specs is None else out_specs,
        scratch_shapes=scratch,
        name=name,
        compiler_params=pltpu.CompilerParams(vmem_limit_bytes=32 << 20),
        cost_estimate=pl.CostEstimate(flops=1 << 28, bytes_accessed=moved, transcendentals=0),
    )


def per_device(source, blocks, columns, rows_up, rows_down):
    count = lax.axis_size("space")
    rows, halo = blocks.shape[0], rows_up.shape[0]
    own, width = rows * BS, halo * BS
    times = source.shape[0] * count
    me = lax.axis_index("space").reshape(1)
    f32 = lambda *shape: jax.ShapeDtypeStruct(shape, jnp.float32)
    bf16 = lambda *shape: jax.ShapeDtypeStruct(shape, jnp.bfloat16)
    tables = [
        jnp.concatenate(halves(jnp.asarray(table, jnp.float32)), axis=0) for table in time_filters(times)
    ]
    inner_pairs = [(i, i ^ 1) for i in range(count)]
    outer_pairs = [pair for i in range(1, count - 1, 2) for pair in ((i, i + 1), (i + 1, i))]

    def swap(inner, outer):
        return lax.ppermute(inner, "space", inner_pairs), lax.ppermute(outer, "space", outer_pairs)

    start = lax.all_to_all(source, "space", split_axis=1, concat_axis=0, tiled=True)
    side = own + 2 * width
    dma = pltpu.SemaphoreType.DMA
    *blocked, place, table = call(
        functools.partial(build_kernel, count),
        (
            *[bf16(SLOTS * BS, own)] * 2,
            *[bf16(2 * BS, 2 * width)] * 2,
            jax.ShapeDtypeStruct((8, 2 * width), jnp.int32),
            jax.ShapeDtypeStruct((SLOTS + 1, rows), jnp.int32),
        ),
        "operator",
        [SMEM] * 4 + [ANY],
        (VMEM,) * 5 + (SMEM,),
        scratch=[pltpu.VMEM(blocks.shape, jnp.float32), dma((rows // 2,))],
        moved=16 << 20,
    )(me, columns.T, rows_up, rows_down, blocks)
    sent = (f32(times, width), f32(times, width))
    value, ahead = f32(times, own), f32(times, 2 * width)

    inner, outer, pick = call(first_kernel, (*sent, bf16(own, 2 * width)), "send_0", [VMEM] * 2)(start, place)
    inner, outer = swap(inner, outer)
    part, part_sent, high, low, *halo_parts = call(
        own_first_kernel,
        (value, ahead, *[bf16(side, own)] * 2, *[bf16(2 * width, 2 * width)] * 2),
        "own_1",
        [VMEM] * 6 + [ANY],
        scratch=[pltpu.SMEM((SLOTS + 1, rows), jnp.int32), dma],
    )(start, *blocked, pick, table)
    next_inner, next_outer = call(send_kernel, sent, "send_1", [VMEM] * 5)(part_sent, inner, outer, *halo_parts)
    next_inner, next_outer = swap(next_inner, next_outer)
    part, part_sent, total = call(own_second_kernel, (value, ahead, value), "own_2", [VMEM] * 9)(
        start, part, inner, outer, high, low, pick, tables[0], tables[1]
    )
    inner, outer = next_inner, next_outer
    next_inner, next_outer = call(send_last_kernel, sent, "send_2", [VMEM] * 6)(
        part_sent, inner, outer, *halo_parts, tables[3]
    )
    next_inner, next_outer = swap(next_inner, next_outer)
    part = call(own_third_kernel, value, "own_3", [VMEM] * 8)(part, inner, outer, total, high, low, tables[2], tables[3])
    timed = call(close_kernel, value, "close", [VMEM] * 5)(part, next_inner, next_outer, high, low)
    return lax.all_to_all(timed, "space", split_axis=0, concat_axis=1, tiled=True)


def solution(mesh):
    placed = (
        P("space", "group"),
        P(("group", "space"), None, None),
        P(("group", "space"), None),
        P(("group", "space")),
        P(("group", "space")),
    )
    return jax.shard_map(
        per_device, mesh=mesh, in_specs=placed, out_specs=P("space", "group"), check_vma=False
    )
```

```python
import functools

import jax
import jax.numpy as jnp
import numpy as np
from jax import lax
from jax.experimental import pallas as pl
from jax.experimental.pallas import tpu as pltpu
from jax.sharding import PartitionSpec as P

BS = 64
SLOTS = 7
SHIFT_SCALE = 2.0
DIAG_CENTER = 4.0
TERMS = 4
VMEM = pl.BlockSpec(memory_space=pltpu.VMEM)
SMEM = pl.BlockSpec(memory_space=pltpu.SMEM)
ANY = pl.BlockSpec(memory_space=pl.ANY)


def time_filters(length):
    phase = np.exp(-2j * np.pi * np.arange(length) / length)
    step = 1.0 / (DIAG_CENTER + SHIFT_SCALE * (1.0 - phase))
    apart = np.arange(length)[:, None] - np.arange(length)[None, :]
    return [np.fft.ifft(step ** (m + 1)).real[apart % length] for m in range(TERMS)]


def halves(value):
    high = value.astype(jnp.bfloat16)
    return high, (value - high.astype(jnp.float32)).astype(jnp.bfloat16)


def mm(left, right):
    return jnp.dot(left, right, preferred_element_type=jnp.float32)


def mm_split(left, right_high, right_low):
    rows = left.shape[0]
    high, low = halves(left)
    both = mm(jnp.concatenate([high, low], axis=0), right_high)
    return both[:rows] + both[rows:] + mm(high, right_low)


def filter_mm(table, value):
    rows = table.shape[0] // 2
    high, low = halves(value)
    both = mm(table, high)
    return both[:rows] + both[rows:] + mm(table[:rows], low)


def chosen(even, up_ref, down_ref, index, halo):
    first = jnp.where(even, up_ref[index % halo], down_ref[index % halo])
    second = jnp.where(even, down_ref[index % halo], up_ref[index % halo])
    return first if index < halo else second


def build_kernel(
    count, me_ref, columns_ref, up_ref, down_ref, blocks_in,
    high_ref, low_ref, sent_high_ref, sent_low_ref, place_ref, table_ref, blocks_ref, block_sems,
):
    rows, size, _ = blocks_ref.shape
    halo = up_ref.shape[0]
    pieces = [
        pltpu.make_async_copy(
            blocks_in.at[pl.ds(2 * pair, 2)], blocks_ref.at[pl.ds(2 * pair, 2)], block_sems.at[pair]
        )
        for pair in range(rows // 2)
    ]
    for copy in pieces:
        copy.start()
    me = me_ref[0]
    even = lax.rem(me, 2) == 0
    sent = [chosen(even, up_ref, down_ref, index, halo) for index in range(2 * halo)]
    for index in range(2 * halo):
        table_ref[SLOTS, index] = sent[index]
    for row in range(rows):
        for slot in range(SLOTS):
            column = columns_ref[slot, row]
            if slot in (1, 2):
                column = jnp.where(even, column + (halo if slot == 1 else -halo), column)
            table_ref[slot, row] = column
    lane = lax.broadcasted_iota(jnp.int32, (size, 2 * size), 1)
    inner = lax.broadcasted_iota(jnp.int32, (size, 2 * size), 0)
    for pair in range(rows // 2):
        pieces[pair].wait()
        lanes = slice(pair * 2 * size, (pair + 1) * 2 * size)
        across = -blocks_ref[2 * pair : 2 * pair + 2].reshape(2 * size, SLOTS * size).T
        part = [across[slot * size : (slot + 1) * size] for slot in range(SLOTS)]
        part[0] = part[0] + jnp.where(lax.rem(lane, size) == inner, DIAG_CENTER, 0.0)
        part[1] = jnp.where(me == 0, 0.0, part[1])
        part[2] = jnp.where(me == count - 1, 0.0, part[2])
        for later in range(3, SLOTS):
            for sooner in (0, *range(3, later)):
                same = [columns_ref[later, 2 * pair + half] == columns_ref[sooner, 2 * pair + half] for half in range(2)]
                moved = jnp.where(lane < size, same[0].astype(jnp.int32), same[1].astype(jnp.int32)) > 0
                part[sooner] = part[sooner] + jnp.where(moved, part[later], 0.0)
                part[later] = jnp.where(moved, 0.0, part[later])
        for slot in range(SLOTS):
            high, low = halves(part[slot])
            high_ref[slot * size : (slot + 1) * size, lanes] = high
            low_ref[slot * size : (slot + 1) * size, lanes] = low
    wide = lax.broadcasted_iota(jnp.int32, (2 * size, 2 * size), 1)
    for pair in range(halo):
        lanes = slice(pair * 2 * size, (pair + 1) * 2 * size)
        for whole_ref, few_ref in ((high_ref, sent_high_ref), (low_ref, sent_low_ref)):
            parts = []
            for half in range(2):
                row = sent[2 * pair + half]
                at = pl.ds(pl.multiple_of((row // 2) * 2 * size, 2 * size), 2 * size)
                tile = whole_ref[size : 3 * size, at].astype(jnp.float32)
                parts.append(jnp.where(lax.rem(row, 2) == half, tile, pltpu.roll(tile, size, 1)))
            few_ref[:, lanes] = jnp.where(wide < size, parts[0], parts[1]).astype(jnp.bfloat16)
        across = lax.broadcasted_iota(jnp.int32, (place_ref.shape[0], 2 * size), 1)
        place_ref[:, lanes] = jnp.where(across < size, sent[2 * pair], sent[2 * pair + 1] - 1) * size + across


def store_sent(value, inner_ref, outer_ref):
    width = inner_ref.shape[1]
    inner_ref[...] = value[:, :width]
    outer_ref[...] = value[:, width:]


def picked(value, pick_ref):
    high, low = halves(value)
    rows = high.shape[0]
    both = mm(jnp.concatenate([high, low], axis=0), pick_ref[...])
    return both[:rows] + both[rows:]


def first_kernel(value_ref, place_ref, inner_ref, outer_ref, pick_ref):
    down = lax.broadcasted_iota(jnp.int32, pick_ref.shape, 0)
    pick_ref[...] = jnp.where(down == place_ref[0:1, :], 1.0, 0.0).astype(jnp.bfloat16)
    store_sent(picked(value_ref[...], pick_ref), inner_ref, outer_ref)


def own_first_kernel(
    value_ref, blocks_high, blocks_low, sent_high, sent_low, pick_ref, table_in,
    out_ref, sent_ref, high_ref, low_ref, halo_high, halo_low, table_ref, sem,
):
    times, own = value_ref.shape
    size = BS
    rows = own // size
    copy = pltpu.make_async_copy(table_in, table_ref, sem)
    copy.start()
    for ref in (high_ref, low_ref, halo_high, halo_low):
        ref[...] = jnp.zeros_like(ref)
    copy.wait()
    for slot in reversed(range(SLOTS)):
        for row in range(rows):
            at = pl.ds(pl.multiple_of(table_ref[slot, row] * size, size), size)
            lanes = slice(row * size, (row + 1) * size)
            high_ref[at, lanes] = blocks_high[slot * size : (slot + 1) * size, lanes]
            low_ref[at, lanes] = blocks_low[slot * size : (slot + 1) * size, lanes]
    for index in range(sent_high.shape[1] // size):
        row = table_ref[SLOTS, index]
        lanes = slice(index * size, (index + 1) * size)
        for slot in (1, 2):
            at = pl.ds(pl.multiple_of((table_ref[slot, row] - rows) * size, size), size)
            halo_high[at, lanes] = sent_high[(slot - 1) * size : slot * size, lanes]
            halo_low[at, lanes] = sent_low[(slot - 1) * size : slot * size, lanes]
    out_ref[...] = mm_split(value_ref[...], high_ref[:own], low_ref[:own])
    sent_ref[...] = picked(out_ref[...], pick_ref)


def halo_once(inner_ref, outer_ref, high):
    both = jnp.concatenate([inner_ref[...], outer_ref[...]], axis=1)
    return mm(both.astype(jnp.bfloat16), high)


def halo_product(inner_ref, outer_ref, high, low):
    both = jnp.concatenate([inner_ref[...], outer_ref[...]], axis=1)
    return mm_split(both, high, low)


def send_kernel(part_ref, from_inner, from_outer, halo_high, halo_low, inner_ref, outer_ref):
    value = part_ref[...] + halo_product(from_inner, from_outer, halo_high[...], halo_low[...])
    store_sent(value, inner_ref, outer_ref)


def send_last_kernel(part_ref, from_inner, from_outer, halo_high, halo_low, table_ref, inner_ref, outer_ref):
    value = part_ref[...] + halo_product(from_inner, from_outer, halo_high[...], halo_low[...])
    table = table_ref[: value.shape[0]]
    store_sent(mm(table, value.astype(jnp.bfloat16)), inner_ref, outer_ref)


def own_second_kernel(
    start_ref, part_ref, from_inner, from_outer, high_ref, low_ref, pick_ref, table0_ref, table1_ref,
    out_ref, sent_ref, total_ref,
):
    own = part_ref.shape[1]
    value = part_ref[...] + halo_product(from_inner, from_outer, high_ref[own:], low_ref[own:])
    out_ref[...] = mm_split(value, high_ref[:own], low_ref[:own])
    sent_ref[...] = picked(out_ref[...], pick_ref)
    total_ref[...] = filter_mm(table0_ref[...], start_ref[...]) + filter_mm(table1_ref[...], value)


def own_third_kernel(part_ref, from_inner, from_outer, total_ref, high_ref, low_ref, table2_ref, table3_ref, out_ref):
    own = part_ref.shape[1]
    value = part_ref[...] + halo_product(from_inner, from_outer, high_ref[own:], low_ref[own:])
    filtered = filter_mm(table3_ref[...], value)
    out_ref[...] = (
        total_ref[...] + filter_mm(table2_ref[...], value) + mm_split(filtered, high_ref[:own], low_ref[:own])
    )


def close_kernel(part_ref, from_inner, from_outer, high_ref, out_ref):
    own = part_ref.shape[1]
    out_ref[...] = part_ref[...] + halo_once(from_inner, from_outer, high_ref[own:])


def call(kernel, outs, name, ins, out_specs=None, scratch=(), moved=4 << 20):
    return pl.pallas_call(
        kernel,
        out_shape=outs,
        in_specs=ins,
        out_specs=jax.tree.map(lambda _: VMEM, outs) if out_specs is None else out_specs,
        scratch_shapes=scratch,
        name=name,
        compiler_params=pltpu.CompilerParams(vmem_limit_bytes=32 << 20),
        cost_estimate=pl.CostEstimate(flops=1 << 28, bytes_accessed=moved, transcendentals=0),
    )


def per_device(source, blocks, columns, rows_up, rows_down):
    count = lax.axis_size("space")
    rows, halo = blocks.shape[0], rows_up.shape[0]
    own, width = rows * BS, halo * BS
    times = source.shape[0] * count
    me = lax.axis_index("space").reshape(1)
    f32 = lambda *shape: jax.ShapeDtypeStruct(shape, jnp.float32)
    bf16 = lambda *shape: jax.ShapeDtypeStruct(shape, jnp.bfloat16)
    tables = [
        jnp.concatenate(halves(jnp.asarray(table, jnp.float32)), axis=0) for table in time_filters(times)
    ]
    inner_pairs = [(i, i ^ 1) for i in range(count)]
    groups = lax.axis_size("group")
    outer_pairs = [
        (group * count + i, group * count + j)
        for group in range(groups)
        for pair in range(1, count - 1, 2)
        for i, j in ((pair, pair + 1), (pair + 1, pair))
    ]
    if groups % 2 == 0:
        outer_pairs += [(group * count + i, (group ^ 1) * count + i) for group in range(groups) for i in (0, count - 1)]

    def swap(inner, outer):
        return lax.ppermute(inner, "space", inner_pairs), lax.ppermute(outer, ("group", "space"), outer_pairs)

    start = lax.all_to_all(source, "space", split_axis=1, concat_axis=0, tiled=True)
    side = own + 2 * width
    dma = pltpu.SemaphoreType.DMA
    *blocked, place, table = call(
        functools.partial(build_kernel, count),
        (
            *[bf16(SLOTS * BS, own)] * 2,
            *[bf16(2 * BS, 2 * width)] * 2,
            jax.ShapeDtypeStruct((8, 2 * width), jnp.int32),
            jax.ShapeDtypeStruct((SLOTS + 1, rows), jnp.int32),
        ),
        "operator",
        [SMEM] * 4 + [ANY],
        (VMEM,) * 5 + (SMEM,),
        scratch=[pltpu.VMEM(blocks.shape, jnp.float32), dma((rows // 2,))],
        moved=16 << 20,
    )(me, columns.T, rows_up, rows_down, blocks)
    sent = (f32(times, width), f32(times, width))
    value, ahead = f32(times, own), f32(times, 2 * width)

    inner, outer, pick = call(first_kernel, (*sent, bf16(own, 2 * width)), "send_0", [VMEM] * 2)(start, place)
    inner, outer = swap(inner, outer)
    part, part_sent, high, low, *halo_parts = call(
        own_first_kernel,
        (value, ahead, *[bf16(side, own)] * 2, *[bf16(2 * width, 2 * width)] * 2),
        "own_1",
        [VMEM] * 6 + [ANY],
        scratch=[pltpu.SMEM((SLOTS + 1, rows), jnp.int32), dma],
    )(start, *blocked, pick, table)
    next_inner, next_outer = call(send_kernel, sent, "send_1", [VMEM] * 5)(part_sent, inner, outer, *halo_parts)
    next_inner, next_outer = swap(next_inner, next_outer)
    part, part_sent, total = call(own_second_kernel, (value, ahead, value), "own_2", [VMEM] * 9)(
        start, part, inner, outer, high, low, pick, tables[0], tables[1]
    )
    inner, outer = next_inner, next_outer
    next_inner, next_outer = call(send_last_kernel, sent, "send_2", [VMEM] * 6)(
        part_sent, inner, outer, *halo_parts, tables[3]
    )
    next_inner, next_outer = swap(next_inner, next_outer)
    part = call(own_third_kernel, value, "own_3", [VMEM] * 8)(part, inner, outer, total, high, low, tables[2], tables[3])
    timed = call(close_kernel, value, "close", [VMEM] * 4)(part, next_inner, next_outer, high)
    return lax.all_to_all(timed, "space", split_axis=0, concat_axis=1, tiled=True)


def solution(mesh):
    placed = (
        P("space", "group"),
        P(("group", "space"), None, None),
        P(("group", "space"), None),
        P(("group", "space")),
        P(("group", "space")),
    )
    return jax.shard_map(
        per_device, mesh=mesh, in_specs=placed, out_specs=P("space", "group"), check_vma=False
    )
```

```python
import functools

import jax
import jax.numpy as jnp
import numpy as np
from jax import lax
from jax.experimental import pallas as pl
from jax.experimental.pallas import tpu as pltpu
from jax.sharding import PartitionSpec as P

BS = 64
SLOTS = 7
SHIFT_SCALE = 2.0
DIAG_CENTER = 4.0
TERMS = 4
SEND_ORDER = (5, 8, 12, 4, 9, 10, 6, 7, 14, 1, 15, 2, 11, 13, 3, 0)
VMEM = pl.BlockSpec(memory_space=pltpu.VMEM)
SMEM = pl.BlockSpec(memory_space=pltpu.SMEM)
ANY = pl.BlockSpec(memory_space=pl.ANY)


def time_filters(length):
    phase = np.exp(-2j * np.pi * np.arange(length) / length)
    step = 1.0 / (DIAG_CENTER + SHIFT_SCALE * (1.0 - phase))
    apart = np.arange(length)[:, None] - np.arange(length)[None, :]
    return [np.fft.ifft(step ** (m + 1)).real[apart % length] for m in range(TERMS)]


def send_order(count):
    return list(SEND_ORDER) if count == len(SEND_ORDER) else list(range(count))


def halves(value):
    high = value.astype(jnp.bfloat16)
    return high, (value - high.astype(jnp.float32)).astype(jnp.bfloat16)


def mm(left, right):
    return jnp.dot(left, right, preferred_element_type=jnp.float32)


def mm_split(left, right_high, right_low):
    rows = left.shape[0]
    high, low = halves(left)
    both = mm(jnp.concatenate([high, low], axis=0), right_high)
    return both[:rows] + both[rows:] + mm(high, right_low)


def filter_mm(table, value):
    rows = table.shape[0] // 2
    high, low = halves(value)
    both = mm(table, high)
    return both[:rows] + both[rows:] + mm(table[:rows], low)


def chosen(even, up_ref, down_ref, index, halo):
    first = jnp.where(even, up_ref[index % halo], down_ref[index % halo])
    second = jnp.where(even, down_ref[index % halo], up_ref[index % halo])
    return first if index < halo else second


def build_kernel(
    count, me_ref, columns_ref, up_ref, down_ref, blocks_in,
    high_ref, low_ref, sent_high_ref, sent_low_ref, place_ref, table_ref, blocks_ref, block_sems,
):
    rows, size, _ = blocks_ref.shape
    halo = up_ref.shape[0]
    pieces = [
        pltpu.make_async_copy(
            blocks_in.at[pl.ds(2 * pair, 2)], blocks_ref.at[pl.ds(2 * pair, 2)], block_sems.at[pair]
        )
        for pair in range(rows // 2)
    ]
    for copy in pieces:
        copy.start()
    me = me_ref[0]
    even = lax.rem(me, 2) == 0
    sent = [chosen(even, up_ref, down_ref, index, halo) for index in range(2 * halo)]
    for index in range(2 * halo):
        table_ref[SLOTS, index] = sent[index]
    for row in range(rows):
        for slot in range(SLOTS):
            column = columns_ref[slot, row]
            if slot in (1, 2):
                column = jnp.where(even, column + (halo if slot == 1 else -halo), column)
            table_ref[slot, row] = column
    lane = lax.broadcasted_iota(jnp.int32, (size, 2 * size), 1)
    inner = lax.broadcasted_iota(jnp.int32, (size, 2 * size), 0)
    for pair in range(rows // 2):
        pieces[pair].wait()
        lanes = slice(pair * 2 * size, (pair + 1) * 2 * size)
        across = -blocks_ref[2 * pair : 2 * pair + 2].reshape(2 * size, SLOTS * size).T
        part = [across[slot * size : (slot + 1) * size] for slot in range(SLOTS)]
        part[0] = part[0] + jnp.where(lax.rem(lane, size) == inner, DIAG_CENTER, 0.0)
        part[1] = jnp.where(me == 0, 0.0, part[1])
        part[2] = jnp.where(me == count - 1, 0.0, part[2])
        for later in range(3, SLOTS):
            for sooner in (0, *range(3, later)):
                same = [columns_ref[later, 2 * pair + half] == columns_ref[sooner, 2 * pair + half] for half in range(2)]
                moved = jnp.where(lane < size, same[0].astype(jnp.int32), same[1].astype(jnp.int32)) > 0
                part[sooner] = part[sooner] + jnp.where(moved, part[later], 0.0)
                part[later] = jnp.where(moved, 0.0, part[later])
        for slot in range(SLOTS):
            high, low = halves(part[slot])
            high_ref[slot * size : (slot + 1) * size, lanes] = high
            low_ref[slot * size : (slot + 1) * size, lanes] = low
    wide = lax.broadcasted_iota(jnp.int32, (2 * size, 2 * size), 1)
    for pair in range(halo):
        lanes = slice(pair * 2 * size, (pair + 1) * 2 * size)
        for whole_ref, few_ref in ((high_ref, sent_high_ref), (low_ref, sent_low_ref)):
            parts = []
            for half in range(2):
                row = sent[2 * pair + half]
                at = pl.ds(pl.multiple_of((row // 2) * 2 * size, 2 * size), 2 * size)
                tile = whole_ref[size : 3 * size, at].astype(jnp.float32)
                parts.append(jnp.where(lax.rem(row, 2) == half, tile, pltpu.roll(tile, size, 1)))
            few_ref[:, lanes] = jnp.where(wide < size, parts[0], parts[1]).astype(jnp.bfloat16)
        across = lax.broadcasted_iota(jnp.int32, (place_ref.shape[0], 2 * size), 1)
        place_ref[:, lanes] = jnp.where(across < size, sent[2 * pair], sent[2 * pair + 1] - 1) * size + across


def store_sent(value, inner_ref, outer_ref):
    width = inner_ref.shape[1]
    inner_ref[...] = value[:, :width]
    outer_ref[...] = value[:, width:]


def picked(value, pick_ref):
    high, low = halves(value)
    rows = high.shape[0]
    both = mm(jnp.concatenate([high, low], axis=0), pick_ref[...])
    return both[:rows] + both[rows:]


def first_kernel(value_ref, place_ref, inner_ref, outer_ref, pick_ref):
    down = lax.broadcasted_iota(jnp.int32, pick_ref.shape, 0)
    pick_ref[...] = jnp.where(down == place_ref[0:1, :], 1.0, 0.0).astype(jnp.bfloat16)
    store_sent(picked(value_ref[...], pick_ref), inner_ref, outer_ref)


def own_first_kernel(
    value_ref, blocks_high, blocks_low, sent_high, sent_low, pick_ref, table_in,
    out_ref, sent_ref, high_ref, low_ref, halo_high, halo_low, table_ref, sem,
):
    times, own = value_ref.shape
    size = BS
    rows = own // size
    copy = pltpu.make_async_copy(table_in, table_ref, sem)
    copy.start()
    for ref in (high_ref, low_ref, halo_high, halo_low):
        ref[...] = jnp.zeros_like(ref)
    copy.wait()
    for slot in reversed(range(SLOTS)):
        for row in range(rows):
            at = pl.ds(pl.multiple_of(table_ref[slot, row] * size, size), size)
            lanes = slice(row * size, (row + 1) * size)
            high_ref[at, lanes] = blocks_high[slot * size : (slot + 1) * size, lanes]
            low_ref[at, lanes] = blocks_low[slot * size : (slot + 1) * size, lanes]
    for index in range(sent_high.shape[1] // size):
        row = table_ref[SLOTS, index]
        lanes = slice(index * size, (index + 1) * size)
        for slot in (1, 2):
            at = pl.ds(pl.multiple_of((table_ref[slot, row] - rows) * size, size), size)
            halo_high[at, lanes] = sent_high[(slot - 1) * size : slot * size, lanes]
            halo_low[at, lanes] = sent_low[(slot - 1) * size : slot * size, lanes]
    out_ref[...] = mm_split(value_ref[...], high_ref[:own], low_ref[:own])
    sent_ref[...] = picked(out_ref[...], pick_ref)


def halo_once(inner_ref, outer_ref, high):
    both = jnp.concatenate([inner_ref[...], outer_ref[...]], axis=1)
    return mm(both.astype(jnp.bfloat16), high)


def halo_product(inner_ref, outer_ref, high, low):
    both = jnp.concatenate([inner_ref[...], outer_ref[...]], axis=1)
    return mm_split(both, high, low)


def send_kernel(part_ref, from_inner, from_outer, halo_high, halo_low, inner_ref, outer_ref):
    value = part_ref[...] + halo_product(from_inner, from_outer, halo_high[...], halo_low[...])
    store_sent(value, inner_ref, outer_ref)


def send_last_kernel(part_ref, from_inner, from_outer, halo_high, halo_low, table_ref, inner_ref, outer_ref):
    value = part_ref[...] + halo_product(from_inner, from_outer, halo_high[...], halo_low[...])
    table = table_ref[: value.shape[0]]
    store_sent(mm(table, value.astype(jnp.bfloat16)), inner_ref, outer_ref)


def own_second_kernel(
    start_ref, part_ref, from_inner, from_outer, high_ref, low_ref, pick_ref, table0_ref, table1_ref,
    out_ref, sent_ref, total_ref,
):
    own = part_ref.shape[1]
    value = part_ref[...] + halo_product(from_inner, from_outer, high_ref[own:], low_ref[own:])
    out_ref[...] = mm_split(value, high_ref[:own], low_ref[:own])
    sent_ref[...] = picked(out_ref[...], pick_ref)
    total_ref[...] = filter_mm(table0_ref[...], start_ref[...]) + filter_mm(table1_ref[...], value)


def own_third_kernel(part_ref, from_inner, from_outer, total_ref, high_ref, low_ref, table2_ref, table3_ref, out_ref):
    own = part_ref.shape[1]
    value = part_ref[...] + halo_product(from_inner, from_outer, high_ref[own:], low_ref[own:])
    filtered = filter_mm(table3_ref[...], value)
    out_ref[...] = (
        total_ref[...] + filter_mm(table2_ref[...], value) + mm_split(filtered, high_ref[:own], low_ref[:own])
    )


def close_kernel(part_ref, from_inner, from_outer, high_ref, out_ref):
    own = part_ref.shape[1]
    out_ref[...] = part_ref[...] + halo_once(from_inner, from_outer, high_ref[own:])


def store_kernel(order, value_ref, out_ref, sems):
    step = value_ref.shape[1] // len(order)
    copies = [
        pltpu.make_async_copy(
            value_ref.at[:, index * step : (index + 1) * step],
            out_ref.at[:, sender * step : (sender + 1) * step],
            sems.at[index],
        )
        for index, sender in enumerate(order)
    ]
    for copy in copies:
        copy.start()
    for copy in copies:
        copy.wait()


def call(kernel, outs, name, ins, out_specs=None, scratch=(), moved=4 << 20):
    return pl.pallas_call(
        kernel,
        out_shape=outs,
        in_specs=ins,
        out_specs=jax.tree.map(lambda _: VMEM, outs) if out_specs is None else out_specs,
        scratch_shapes=scratch,
        name=name,
        compiler_params=pltpu.CompilerParams(vmem_limit_bytes=32 << 20),
        cost_estimate=pl.CostEstimate(flops=1 << 28, bytes_accessed=moved, transcendentals=0),
    )


def per_device(source, blocks, columns, rows_up, rows_down):
    count = lax.axis_size("space")
    rows, halo = blocks.shape[0], rows_up.shape[0]
    own, width = rows * BS, halo * BS
    times = source.shape[0] * count
    me = lax.axis_index("space").reshape(1)
    f32 = lambda *shape: jax.ShapeDtypeStruct(shape, jnp.float32)
    bf16 = lambda *shape: jax.ShapeDtypeStruct(shape, jnp.bfloat16)
    order = send_order(count)
    told = np.arange(times).reshape(count, -1)[np.array(order)].reshape(-1)
    tables = [
        jnp.concatenate(halves(jnp.asarray(table[told], jnp.float32)), axis=0) for table in time_filters(times)
    ]
    inner_pairs = [(i, i ^ 1) for i in range(count)]
    groups = lax.axis_size("group")
    outer_pairs = [
        (group * count + i, group * count + j)
        for group in range(groups)
        for pair in range(1, count - 1, 2)
        for i, j in ((pair, pair + 1), (pair + 1, pair))
    ]
    if groups % 2 == 0:
        outer_pairs += [(group * count + i, (group ^ 1) * count + i) for group in range(groups) for i in (0, count - 1)]

    def swap(inner, outer):
        return lax.ppermute(inner, "space", inner_pairs), lax.ppermute(outer, ("group", "space"), outer_pairs)

    start = lax.all_to_all(source, "space", split_axis=1, concat_axis=0, tiled=True)
    side = own + 2 * width
    dma = pltpu.SemaphoreType.DMA
    *blocked, place, table = call(
        functools.partial(build_kernel, count),
        (
            *[bf16(SLOTS * BS, own)] * 2,
            *[bf16(2 * BS, 2 * width)] * 2,
            jax.ShapeDtypeStruct((8, 2 * width), jnp.int32),
            jax.ShapeDtypeStruct((SLOTS + 1, rows), jnp.int32),
        ),
        "operator",
        [SMEM] * 4 + [ANY],
        (VMEM,) * 5 + (SMEM,),
        scratch=[pltpu.VMEM(blocks.shape, jnp.float32), dma((rows // 2,))],
        moved=16 << 20,
    )(me, columns.T, rows_up, rows_down, blocks)
    sent = (f32(times, width), f32(times, width))
    value, ahead = f32(times, own), f32(times, 2 * width)

    inner, outer, pick = call(first_kernel, (*sent, bf16(own, 2 * width)), "send_0", [VMEM] * 2)(start, place)
    inner, outer = swap(inner, outer)
    part, part_sent, high, low, *halo_parts = call(
        own_first_kernel,
        (value, ahead, *[bf16(side, own)] * 2, *[bf16(2 * width, 2 * width)] * 2),
        "own_1",
        [VMEM] * 6 + [ANY],
        scratch=[pltpu.SMEM((SLOTS + 1, rows), jnp.int32), dma],
    )(start, *blocked, pick, table)
    next_inner, next_outer = call(send_kernel, sent, "send_1", [VMEM] * 5)(part_sent, inner, outer, *halo_parts)
    next_inner, next_outer = swap(next_inner, next_outer)
    part, part_sent, total = call(own_second_kernel, (value, ahead, value), "own_2", [VMEM] * 9)(
        start, part, inner, outer, high, low, pick, tables[0], tables[1]
    )
    inner, outer = next_inner, next_outer
    next_inner, next_outer = call(send_last_kernel, sent, "send_2", [VMEM] * 6)(
        part_sent, inner, outer, *halo_parts, tables[3]
    )
    next_inner, next_outer = swap(next_inner, next_outer)
    part = call(own_third_kernel, value, "own_3", [VMEM] * 8)(part, inner, outer, total, high, low, tables[2], tables[3])
    timed = call(close_kernel, value, "close", [VMEM] * 4)(part, next_inner, next_outer, high)
    field = lax.all_to_all(
        timed, "space", split_axis=0, concat_axis=1, tiled=True, axis_index_groups=[order]
    )
    return call(
        functools.partial(store_kernel, order),
        jax.ShapeDtypeStruct(field.shape, field.dtype),
        "store",
        [VMEM],
        ANY,
        scratch=[pltpu.SemaphoreType.DMA((count,))],
    )(field)


def solution(mesh):
    placed = (
        P("space", "group"),
        P(("group", "space"), None, None),
        P(("group", "space"), None),
        P(("group", "space")),
        P(("group", "space")),
    )
    return jax.shard_map(
        per_device, mesh=mesh, in_specs=placed, out_specs=P("space", "group"), check_vma=False
    )
```

```python
import functools

import jax
import jax.numpy as jnp
import numpy as np
from jax import lax
from jax.experimental import pallas as pl
from jax.experimental.pallas import tpu as pltpu
from jax.sharding import PartitionSpec as P

BS = 64
SLOTS = 7
SHIFT_SCALE = 2.0
DIAG_CENTER = 4.0
TERMS = 4
SEND_ORDER = (5, 8, 12, 4, 9, 10, 6, 7, 14, 1, 15, 2, 11, 13, 3, 0)
VMEM = pl.BlockSpec(memory_space=pltpu.VMEM)
SMEM = pl.BlockSpec(memory_space=pltpu.SMEM)
ANY = pl.BlockSpec(memory_space=pl.ANY)


def time_filters(length):
    phase = np.exp(-2j * np.pi * np.arange(length) / length)
    step = 1.0 / (DIAG_CENTER + SHIFT_SCALE * (1.0 - phase))
    apart = np.arange(length)[:, None] - np.arange(length)[None, :]
    return [np.fft.ifft(step ** (m + 1)).real[apart % length] for m in range(TERMS)]


def send_order(count):
    return list(SEND_ORDER) if count == len(SEND_ORDER) else list(range(count))


def halves(value):
    high = value.astype(jnp.bfloat16)
    return high, (value - high.astype(jnp.float32)).astype(jnp.bfloat16)


def mm(left, right):
    return jnp.dot(left, right, preferred_element_type=jnp.float32)


def mm_split(left, right_high, right_low):
    rows = left.shape[0]
    high, low = halves(left)
    both = mm(jnp.concatenate([high, low], axis=0), right_high)
    return both[:rows] + both[rows:] + mm(high, right_low)


def filter_mm(table, value):
    rows = table.shape[0] // 2
    high, low = halves(value)
    both = mm(table, high)
    return both[:rows] + both[rows:] + mm(table[:rows], low)


def chosen(even, up_ref, down_ref, index, halo):
    first = jnp.where(even, up_ref[index % halo], down_ref[index % halo])
    second = jnp.where(even, down_ref[index % halo], up_ref[index % halo])
    return first if index < halo else second


def build_kernel(
    count, me_ref, columns_ref, up_ref, down_ref, blocks_in,
    high_ref, low_ref, pick_ref, table_ref, blocks_ref, block_sems,
):
    rows, size, _ = blocks_ref.shape
    halo = up_ref.shape[0]
    pieces = [
        pltpu.make_async_copy(
            blocks_in.at[pl.ds(2 * pair, 2)], blocks_ref.at[pl.ds(2 * pair, 2)], block_sems.at[pair]
        )
        for pair in range(rows // 2)
    ]
    for copy in pieces:
        copy.start()
    me = me_ref[0]
    even = lax.rem(me, 2) == 0
    sent = [chosen(even, up_ref, down_ref, index, halo) for index in range(2 * halo)]
    for index in range(2 * halo):
        table_ref[SLOTS, index] = sent[index]
    for row in range(rows):
        for slot in range(SLOTS):
            column = columns_ref[slot, row]
            if slot in (1, 2):
                column = jnp.where(even, column + (halo if slot == 1 else -halo), column)
            table_ref[slot, row] = column
    lane = lax.broadcasted_iota(jnp.int32, (size, 2 * size), 1)
    inner = lax.broadcasted_iota(jnp.int32, (size, 2 * size), 0)
    for pair in range(rows // 2):
        pieces[pair].wait()
        lanes = slice(pair * 2 * size, (pair + 1) * 2 * size)
        across = -blocks_ref[2 * pair : 2 * pair + 2].reshape(2 * size, SLOTS * size).T
        part = [across[slot * size : (slot + 1) * size] for slot in range(SLOTS)]
        part[0] = part[0] + jnp.where(lax.rem(lane, size) == inner, DIAG_CENTER, 0.0)
        part[1] = jnp.where(me == 0, 0.0, part[1])
        part[2] = jnp.where(me == count - 1, 0.0, part[2])
        for later in range(3, SLOTS):
            for sooner in (0, *range(3, later)):
                same = [columns_ref[later, 2 * pair + half] == columns_ref[sooner, 2 * pair + half] for half in range(2)]
                moved = jnp.where(lane < size, same[0].astype(jnp.int32), same[1].astype(jnp.int32)) > 0
                part[sooner] = part[sooner] + jnp.where(moved, part[later], 0.0)
                part[later] = jnp.where(moved, 0.0, part[later])
        for slot in range(SLOTS):
            high, low = halves(part[slot])
            high_ref[slot * size : (slot + 1) * size, lanes] = high
            low_ref[slot * size : (slot + 1) * size, lanes] = low
    down = lax.broadcasted_iota(jnp.int32, (rows * size, 2 * size), 0)
    across = lax.broadcasted_iota(jnp.int32, (rows * size, 2 * size), 1)
    for pair in range(halo):
        place = jnp.where(across < size, sent[2 * pair], sent[2 * pair + 1] - 1) * size + across
        pick_ref[:, pair * 2 * size : (pair + 1) * 2 * size] = jnp.where(down == place, 1.0, 0.0).astype(jnp.bfloat16)


def store_sent(value, inner_ref, outer_ref):
    width = inner_ref.shape[1]
    inner_ref[...] = value[:, :width]
    outer_ref[...] = value[:, width:]


def picked(value, pick_ref):
    high, low = halves(value)
    rows = high.shape[0]
    both = mm(jnp.concatenate([high, low], axis=0), pick_ref[...])
    return both[:rows] + both[rows:]


def first_kernel(value_ref, pick_ref, inner_ref, outer_ref):
    store_sent(picked(value_ref[...], pick_ref), inner_ref, outer_ref)


def own_first_kernel(
    value_ref, blocks_high, blocks_low, pick_ref, table_in,
    out_ref, sent_ref, high_ref, low_ref, halo_high, halo_low, table_ref, sem,
):
    times, own = value_ref.shape
    size = BS
    rows = own // size
    copy = pltpu.make_async_copy(table_in, table_ref, sem)
    copy.start()
    for ref in (high_ref, low_ref, halo_high, halo_low):
        ref[...] = jnp.zeros_like(ref)
    copy.wait()
    for slot in reversed(range(SLOTS)):
        for row in range(rows):
            at = pl.ds(pl.multiple_of(table_ref[slot, row] * size, size), size)
            lanes = slice(row * size, (row + 1) * size)
            high_ref[at, lanes] = blocks_high[slot * size : (slot + 1) * size, lanes]
            low_ref[at, lanes] = blocks_low[slot * size : (slot + 1) * size, lanes]
    for index in range(sent_ref.shape[1] // size):
        row = table_ref[SLOTS, index]
        half = index % 2
        pair = pl.ds(pl.multiple_of((row // 2) * 2 * size, 2 * size), 2 * size)
        for slot in (1, 2):
            at = pl.ds(pl.multiple_of((table_ref[slot, row] - rows) * size, size), size)
            for whole_ref, few_ref in ((blocks_high, halo_high), (blocks_low, halo_low)):
                tile = whole_ref[slot * size : (slot + 1) * size, pair].astype(jnp.float32)
                tile = jnp.where(lax.rem(row, 2) == half, tile, pltpu.roll(tile, size, 1)).astype(jnp.bfloat16)
                few_ref[at, index * size : (index + 1) * size] = tile[:, half * size : (half + 1) * size]
    out_ref[...] = mm_split(value_ref[...], high_ref[:own], low_ref[:own])
    sent_ref[...] = picked(out_ref[...], pick_ref)


def halo_once(inner_ref, outer_ref, high):
    both = jnp.concatenate([inner_ref[...], outer_ref[...]], axis=1)
    return mm(both.astype(jnp.bfloat16), high)


def halo_product(inner_ref, outer_ref, high, low):
    both = jnp.concatenate([inner_ref[...], outer_ref[...]], axis=1)
    return mm_split(both, high, low)


def send_kernel(part_ref, from_inner, from_outer, halo_high, halo_low, inner_ref, outer_ref):
    value = part_ref[...] + halo_product(from_inner, from_outer, halo_high[...], halo_low[...])
    store_sent(value, inner_ref, outer_ref)


def send_last_kernel(part_ref, from_inner, from_outer, halo_high, table_ref, inner_ref, outer_ref):
    value = part_ref[...] + halo_once(from_inner, from_outer, halo_high[...])
    table = table_ref[: value.shape[0]]
    store_sent(mm(table, value.astype(jnp.bfloat16)), inner_ref, outer_ref)


def own_second_kernel(
    start_ref, part_ref, from_inner, from_outer, high_ref, low_ref, pick_ref, table0_ref, table1_ref,
    out_ref, sent_ref, total_ref,
):
    own = part_ref.shape[1]
    value = part_ref[...] + halo_product(from_inner, from_outer, high_ref[own:], low_ref[own:])
    out_ref[...] = mm_split(value, high_ref[:own], low_ref[:own])
    sent_ref[...] = picked(out_ref[...], pick_ref)
    total_ref[...] = filter_mm(table0_ref[...], start_ref[...]) + filter_mm(table1_ref[...], value)


def own_third_kernel(part_ref, from_inner, from_outer, total_ref, high_ref, low_ref, table2_ref, table3_ref, out_ref):
    own = part_ref.shape[1]
    value = part_ref[...] + halo_product(from_inner, from_outer, high_ref[own:], low_ref[own:])
    filtered = filter_mm(table3_ref[...], value)
    out_ref[...] = (
        total_ref[...] + filter_mm(table2_ref[...], value) + mm_split(filtered, high_ref[:own], low_ref[:own])
    )


def close_kernel(part_ref, from_inner, from_outer, high_ref, out_ref):
    own = part_ref.shape[1]
    out_ref[...] = part_ref[...] + halo_once(from_inner, from_outer, high_ref[own:])


def store_kernel(order, value_ref, out_ref, sems):
    step = value_ref.shape[1] // len(order)
    copies = [
        pltpu.make_async_copy(
            value_ref.at[:, index * step : (index + 1) * step],
            out_ref.at[:, sender * step : (sender + 1) * step],
            sems.at[index],
        )
        for index, sender in enumerate(order)
    ]
    for copy in copies:
        copy.start()
    for copy in copies:
        copy.wait()


def call(kernel, outs, name, ins, out_specs=None, scratch=(), moved=4 << 20):
    return pl.pallas_call(
        kernel,
        out_shape=outs,
        in_specs=ins,
        out_specs=jax.tree.map(lambda _: VMEM, outs) if out_specs is None else out_specs,
        scratch_shapes=scratch,
        name=name,
        compiler_params=pltpu.CompilerParams(vmem_limit_bytes=32 << 20),
        cost_estimate=pl.CostEstimate(flops=1 << 28, bytes_accessed=moved, transcendentals=0),
    )


def per_device(source, blocks, columns, rows_up, rows_down):
    count = lax.axis_size("space")
    rows, halo = blocks.shape[0], rows_up.shape[0]
    own, width = rows * BS, halo * BS
    times = source.shape[0] * count
    me = lax.axis_index("space").reshape(1)
    f32 = lambda *shape: jax.ShapeDtypeStruct(shape, jnp.float32)
    bf16 = lambda *shape: jax.ShapeDtypeStruct(shape, jnp.bfloat16)
    order = send_order(count)
    told = np.arange(times).reshape(count, -1)[np.array(order)].reshape(-1)
    tables = [
        jnp.concatenate(halves(jnp.asarray(table[told], jnp.float32)), axis=0) for table in time_filters(times)
    ]
    inner_pairs = [(i, i ^ 1) for i in range(count)]
    groups = lax.axis_size("group")
    outer_pairs = [
        (group * count + i, group * count + j)
        for group in range(groups)
        for pair in range(1, count - 1, 2)
        for i, j in ((pair, pair + 1), (pair + 1, pair))
    ]
    if groups % 2 == 0:
        outer_pairs += [(group * count + i, (group ^ 1) * count + i) for group in range(groups) for i in (0, count - 1)]

    def swap(inner, outer):
        return lax.ppermute(inner, "space", inner_pairs), lax.ppermute(outer, ("group", "space"), outer_pairs)

    start = lax.all_to_all(source, "space", split_axis=1, concat_axis=0, tiled=True)
    side = own + 2 * width
    dma = pltpu.SemaphoreType.DMA
    *blocked, pick, table = call(
        functools.partial(build_kernel, count),
        (
            *[bf16(SLOTS * BS, own)] * 2,
            bf16(own, 2 * width),
            jax.ShapeDtypeStruct((SLOTS + 1, rows), jnp.int32),
        ),
        "operator",
        [SMEM] * 4 + [ANY],
        (VMEM,) * 3 + (SMEM,),
        scratch=[pltpu.VMEM(blocks.shape, jnp.float32), dma((rows // 2,))],
        moved=16 << 20,
    )(me, columns.T, rows_up, rows_down, blocks)
    sent = (f32(times, width), f32(times, width))
    value, ahead = f32(times, own), f32(times, 2 * width)

    inner, outer = call(first_kernel, sent, "send_0", [VMEM] * 2)(start, pick)
    inner, outer = swap(inner, outer)
    part, part_sent, high, low, *halo_parts = call(
        own_first_kernel,
        (value, ahead, *[bf16(side, own)] * 2, *[bf16(2 * width, 2 * width)] * 2),
        "own_1",
        [VMEM] * 4 + [ANY],
        scratch=[pltpu.SMEM((SLOTS + 1, rows), jnp.int32), dma],
    )(start, *blocked, pick, table)
    next_inner, next_outer = call(send_kernel, sent, "send_1", [VMEM] * 5)(part_sent, inner, outer, *halo_parts)
    next_inner, next_outer = swap(next_inner, next_outer)
    part, part_sent, total = call(own_second_kernel, (value, ahead, value), "own_2", [VMEM] * 9)(
        start, part, inner, outer, high, low, pick, tables[0], tables[1]
    )
    inner, outer = next_inner, next_outer
    next_inner, next_outer = call(send_last_kernel, sent, "send_2", [VMEM] * 5)(
        part_sent, inner, outer, halo_parts[0], tables[3]
    )
    next_inner, next_outer = swap(next_inner, next_outer)
    part = call(own_third_kernel, value, "own_3", [VMEM] * 8)(part, inner, outer, total, high, low, tables[2], tables[3])
    timed = call(close_kernel, value, "close", [VMEM] * 4)(part, next_inner, next_outer, high)
    field = lax.all_to_all(
        timed, "space", split_axis=0, concat_axis=1, tiled=True, axis_index_groups=[order]
    )
    return call(
        functools.partial(store_kernel, order),
        jax.ShapeDtypeStruct(field.shape, field.dtype),
        "store",
        [VMEM],
        ANY,
        scratch=[pltpu.SemaphoreType.DMA((count,))],
    )(field)


def solution(mesh):
    placed = (
        P("space", "group"),
        P(("group", "space"), None, None),
        P(("group", "space"), None),
        P(("group", "space")),
        P(("group", "space")),
    )
    return jax.shard_map(
        per_device, mesh=mesh, in_specs=placed, out_specs=P("space", "group"), check_vma=False
    )
```

```python
import functools

import jax
import jax.numpy as jnp
import numpy as np
from jax import lax
from jax.experimental import pallas as pl
from jax.experimental.pallas import tpu as pltpu
from jax.sharding import PartitionSpec as P

BS = 64
SLOTS = 7
SHIFT_SCALE = 2.0
DIAG_CENTER = 4.0
TERMS = 4
SEND_ORDER = (5, 8, 12, 4, 9, 10, 6, 7, 14, 1, 15, 2, 11, 13, 3, 0)
VMEM = pl.BlockSpec(memory_space=pltpu.VMEM)
SMEM = pl.BlockSpec(memory_space=pltpu.SMEM)
ANY = pl.BlockSpec(memory_space=pl.ANY)


def time_filters(length):
    phase = np.exp(-2j * np.pi * np.arange(length) / length)
    step = 1.0 / (DIAG_CENTER + SHIFT_SCALE * (1.0 - phase))
    apart = np.arange(length)[:, None] - np.arange(length)[None, :]
    return [np.fft.ifft(step ** (m + 1)).real[apart % length] for m in range(TERMS)]


def send_order(count):
    return list(SEND_ORDER) if count == len(SEND_ORDER) else list(range(count))


def halves(value):
    high = value.astype(jnp.bfloat16)
    return high, (value - high.astype(jnp.float32)).astype(jnp.bfloat16)


def mm(left, right):
    return jnp.dot(left, right, preferred_element_type=jnp.float32)


def mm_split(left, right_high, right_low):
    rows = left.shape[0]
    high, low = halves(left)
    both = mm(jnp.concatenate([high, low], axis=0), right_high)
    return both[:rows] + both[rows:] + mm(high, right_low)


def filter_mm(table, value):
    rows = table.shape[0] // 2
    high, low = halves(value)
    both = mm(table, high)
    return both[:rows] + both[rows:] + mm(table[:rows], low)


def chosen(even, up_ref, down_ref, index, halo):
    first = jnp.where(even, up_ref[index % halo], down_ref[index % halo])
    second = jnp.where(even, down_ref[index % halo], up_ref[index % halo])
    return first if index < halo else second


def build_kernel(
    count, me_ref, columns_ref, up_ref, down_ref, blocks_in,
    high_ref, low_ref, pick_ref, table_ref, blocks_ref, block_sems,
):
    rows, size, _ = blocks_ref.shape
    halo = up_ref.shape[0]
    pieces = [
        pltpu.make_async_copy(
            blocks_in.at[pl.ds(2 * pair, 2)], blocks_ref.at[pl.ds(2 * pair, 2)], block_sems.at[pair]
        )
        for pair in range(rows // 2)
    ]
    for copy in pieces:
        copy.start()
    me = me_ref[0]
    even = lax.rem(me, 2) == 0
    sent = [chosen(even, up_ref, down_ref, index, halo) for index in range(2 * halo)]
    for index in range(2 * halo):
        table_ref[SLOTS, index] = sent[index]
    for row in range(rows):
        for slot in range(SLOTS):
            column = columns_ref[slot, row]
            if slot in (1, 2):
                column = jnp.where(even, column + (halo if slot == 1 else -halo), column)
            table_ref[slot, row] = column
    lane = lax.broadcasted_iota(jnp.int32, (size, 2 * size), 1)
    inner = lax.broadcasted_iota(jnp.int32, (size, 2 * size), 0)
    for pair in range(rows // 2):
        pieces[pair].wait()
        lanes = slice(pair * 2 * size, (pair + 1) * 2 * size)
        across = -blocks_ref[2 * pair : 2 * pair + 2].reshape(2 * size, SLOTS * size).T
        part = [across[slot * size : (slot + 1) * size] for slot in range(SLOTS)]
        part[0] = part[0] + jnp.where(lax.rem(lane, size) == inner, DIAG_CENTER, 0.0)
        part[1] = jnp.where(me == 0, 0.0, part[1])
        part[2] = jnp.where(me == count - 1, 0.0, part[2])
        for later in range(3, SLOTS):
            for sooner in (0, *range(3, later)):
                same = [columns_ref[later, 2 * pair + half] == columns_ref[sooner, 2 * pair + half] for half in range(2)]
                moved = jnp.where(lane < size, same[0].astype(jnp.int32), same[1].astype(jnp.int32)) > 0
                part[sooner] = part[sooner] + jnp.where(moved, part[later], 0.0)
                part[later] = jnp.where(moved, 0.0, part[later])
        for slot in range(SLOTS):
            high, low = halves(part[slot])
            high_ref[slot * size : (slot + 1) * size, lanes] = high
            low_ref[slot * size : (slot + 1) * size, lanes] = low
    down = lax.broadcasted_iota(jnp.int32, (rows * size, 2 * size), 0)
    across = lax.broadcasted_iota(jnp.int32, (rows * size, 2 * size), 1)
    for pair in range(halo):
        place = jnp.where(across < size, sent[2 * pair], sent[2 * pair + 1] - 1) * size + across
        pick_ref[:, pair * 2 * size : (pair + 1) * 2 * size] = jnp.where(down == place, 1.0, 0.0).astype(jnp.bfloat16)


def store_sent(value, inner_ref, outer_ref):
    width = inner_ref.shape[1]
    inner_ref[...] = value[:, :width]
    outer_ref[...] = value[:, width:]


def picked(value, pick_ref):
    high, low = halves(value)
    rows = high.shape[0]
    both = mm(jnp.concatenate([high, low], axis=0), pick_ref[...])
    return both[:rows] + both[rows:]


def first_kernel(value_ref, pick_ref, inner_ref, outer_ref):
    store_sent(picked(value_ref[...], pick_ref), inner_ref, outer_ref)


def own_first_kernel(
    value_ref, blocks_high, blocks_low, pick_ref, table_in,
    out_ref, sent_ref, high_ref, low_ref, halo_high, halo_low, table_ref, sem,
):
    times, own = value_ref.shape
    size = BS
    rows = own // size
    copy = pltpu.make_async_copy(table_in, table_ref, sem)
    copy.start()
    for ref in (high_ref, low_ref, halo_high, halo_low):
        ref[...] = jnp.zeros_like(ref)
    copy.wait()
    for slot in reversed(range(SLOTS)):
        for row in range(rows):
            at = pl.ds(pl.multiple_of(table_ref[slot, row] * size, size), size)
            lanes = slice(row * size, (row + 1) * size)
            high_ref[at, lanes] = blocks_high[slot * size : (slot + 1) * size, lanes]
            low_ref[at, lanes] = blocks_low[slot * size : (slot + 1) * size, lanes]
    for index in range(sent_ref.shape[1] // size):
        row = table_ref[SLOTS, index]
        half = index % 2
        pair = pl.ds(pl.multiple_of((row // 2) * 2 * size, 2 * size), 2 * size)
        for slot in (1, 2):
            at = pl.ds(pl.multiple_of((table_ref[slot, row] - rows) * size, size), size)
            for whole_ref, few_ref in ((blocks_high, halo_high), (blocks_low, halo_low)):
                tile = whole_ref[slot * size : (slot + 1) * size, pair].astype(jnp.float32)
                tile = jnp.where(lax.rem(row, 2) == half, tile, pltpu.roll(tile, size, 1)).astype(jnp.bfloat16)
                few_ref[at, index * size : (index + 1) * size] = tile[:, half * size : (half + 1) * size]
    out_ref[...] = mm_split(value_ref[...], high_ref[:own], low_ref[:own])
    sent_ref[...] = picked(out_ref[...], pick_ref)


def halo_once(inner_ref, outer_ref, high):
    both = jnp.concatenate([inner_ref[...], outer_ref[...]], axis=1)
    return mm(both.astype(jnp.bfloat16), high)


def halo_product(inner_ref, outer_ref, high, low):
    both = jnp.concatenate([inner_ref[...], outer_ref[...]], axis=1)
    return mm_split(both, high, low)


def send_kernel(part_ref, from_inner, from_outer, halo_high, halo_low, inner_ref, outer_ref):
    value = part_ref[...] + halo_product(from_inner, from_outer, halo_high[...], halo_low[...])
    store_sent(value, inner_ref, outer_ref)


def send_last_kernel(part_ref, from_inner, from_outer, halo_high, table_ref, inner_ref, outer_ref):
    value = part_ref[...] + halo_once(from_inner, from_outer, halo_high[...])
    table = table_ref[: value.shape[0]]
    store_sent(mm(table, value.astype(jnp.bfloat16)), inner_ref, outer_ref)


def own_second_kernel(
    start_ref, part_ref, from_inner, from_outer, high_ref, low_ref, pick_ref, table0_ref, table1_ref,
    out_ref, sent_ref, total_ref,
):
    own = part_ref.shape[1]
    value = part_ref[...] + halo_product(from_inner, from_outer, high_ref[own:], low_ref[own:])
    out_ref[...] = mm_split(value, high_ref[:own], low_ref[:own])
    sent_ref[...] = picked(out_ref[...], pick_ref)
    total_ref[...] = filter_mm(table0_ref[...], start_ref[...]) + filter_mm(table1_ref[...], value)


def own_third_kernel(part_ref, from_inner, from_outer, total_ref, high_ref, low_ref, table2_ref, table3_ref, out_ref):
    own = part_ref.shape[1]
    value = part_ref[...] + halo_product(from_inner, from_outer, high_ref[own:], low_ref[own:])
    filtered = filter_mm(table3_ref[...], value)
    out_ref[...] = (
        total_ref[...] + filter_mm(table2_ref[...], value) + mm_split(filtered, high_ref[:own], low_ref[:own])
    )


def close_kernel(part_ref, from_inner, from_outer, high_ref, out_ref):
    own = part_ref.shape[1]
    out_ref[...] = part_ref[...] + halo_once(from_inner, from_outer, high_ref[own:])


def store_kernel(order, value_ref, out_ref, sem):
    step = value_ref.shape[1] // len(order)
    copies = [
        pltpu.make_async_copy(
            value_ref.at[:, index * step : (index + 1) * step],
            out_ref.at[:, sender * step : (sender + 1) * step],
            sem,
        )
        for index, sender in enumerate(order)
    ]
    for copy in copies:
        copy.start()
    pltpu.make_async_copy(value_ref, out_ref, sem).wait()


def call(kernel, outs, name, ins, out_specs=None, scratch=(), moved=4 << 20):
    return pl.pallas_call(
        kernel,
        out_shape=outs,
        in_specs=ins,
        out_specs=jax.tree.map(lambda _: VMEM, outs) if out_specs is None else out_specs,
        scratch_shapes=scratch,
        name=name,
        compiler_params=pltpu.CompilerParams(vmem_limit_bytes=32 << 20),
        cost_estimate=pl.CostEstimate(flops=1 << 28, bytes_accessed=moved, transcendentals=0),
    )


def per_device(source, blocks, columns, rows_up, rows_down):
    count = lax.axis_size("space")
    rows, halo = blocks.shape[0], rows_up.shape[0]
    own, width = rows * BS, halo * BS
    times = source.shape[0] * count
    me = lax.axis_index("space").reshape(1)
    f32 = lambda *shape: jax.ShapeDtypeStruct(shape, jnp.float32)
    bf16 = lambda *shape: jax.ShapeDtypeStruct(shape, jnp.bfloat16)
    order = send_order(count)
    told = np.arange(times).reshape(count, -1)[np.array(order)].reshape(-1)
    tables = [
        jnp.concatenate(halves(jnp.asarray(table[told], jnp.float32)), axis=0) for table in time_filters(times)
    ]
    inner_pairs = [(i, i ^ 1) for i in range(count)]
    groups = lax.axis_size("group")
    outer_pairs = [
        (group * count + i, group * count + j)
        for group in range(groups)
        for pair in range(1, count - 1, 2)
        for i, j in ((pair, pair + 1), (pair + 1, pair))
    ]
    if groups % 2 == 0:
        outer_pairs += [(group * count + i, (group ^ 1) * count + i) for group in range(groups) for i in (0, count - 1)]

    def swap(inner, outer):
        return lax.ppermute(inner, "space", inner_pairs), lax.ppermute(outer, ("group", "space"), outer_pairs)

    start = lax.all_to_all(source, "space", split_axis=1, concat_axis=0, tiled=True)
    side = own + 2 * width
    dma = pltpu.SemaphoreType.DMA
    *blocked, pick, table = call(
        functools.partial(build_kernel, count),
        (
            *[bf16(SLOTS * BS, own)] * 2,
            bf16(own, 2 * width),
            jax.ShapeDtypeStruct((SLOTS + 1, rows), jnp.int32),
        ),
        "operator",
        [SMEM] * 4 + [ANY],
        (VMEM,) * 3 + (SMEM,),
        scratch=[pltpu.VMEM(blocks.shape, jnp.float32), dma((rows // 2,))],
        moved=16 << 20,
    )(me, columns.T, rows_up, rows_down, blocks)
    sent = (f32(times, width), f32(times, width))
    value, ahead = f32(times, own), f32(times, 2 * width)

    inner, outer = call(first_kernel, sent, "send_0", [VMEM] * 2)(start, pick)
    inner, outer = swap(inner, outer)
    part, part_sent, high, low, *halo_parts = call(
        own_first_kernel,
        (value, ahead, *[bf16(side, own)] * 2, *[bf16(2 * width, 2 * width)] * 2),
        "own_1",
        [VMEM] * 4 + [ANY],
        scratch=[pltpu.SMEM((SLOTS + 1, rows), jnp.int32), dma],
    )(start, *blocked, pick, table)
    next_inner, next_outer = call(send_kernel, sent, "send_1", [VMEM] * 5)(part_sent, inner, outer, *halo_parts)
    next_inner, next_outer = swap(next_inner, next_outer)
    part, part_sent, total = call(own_second_kernel, (value, ahead, value), "own_2", [VMEM] * 9)(
        start, part, inner, outer, high, low, pick, tables[0], tables[1]
    )
    inner, outer = next_inner, next_outer
    next_inner, next_outer = call(send_last_kernel, sent, "send_2", [VMEM] * 5)(
        part_sent, inner, outer, halo_parts[0], tables[3]
    )
    next_inner, next_outer = swap(next_inner, next_outer)
    part = call(own_third_kernel, value, "own_3", [VMEM] * 8)(part, inner, outer, total, high, low, tables[2], tables[3])
    timed = call(close_kernel, value, "close", [VMEM] * 4)(part, next_inner, next_outer, high)
    field = lax.all_to_all(
        timed, "space", split_axis=0, concat_axis=1, tiled=True, axis_index_groups=[order]
    )
    return call(
        functools.partial(store_kernel, order),
        jax.ShapeDtypeStruct(field.shape, field.dtype),
        "store",
        [VMEM],
        ANY,
        scratch=[pltpu.SemaphoreType.DMA],
    )(field)


def solution(mesh):
    placed = (
        P("space", "group"),
        P(("group", "space"), None, None),
        P(("group", "space"), None),
        P(("group", "space")),
        P(("group", "space")),
    )
    return jax.shard_map(
        per_device, mesh=mesh, in_specs=placed, out_specs=P("space", "group"), check_vma=False
    )
```

```python
import functools

import jax
import jax.numpy as jnp
import numpy as np
from jax import lax
from jax.experimental import pallas as pl
from jax.experimental.pallas import tpu as pltpu
from jax.sharding import PartitionSpec as P

BS = 64
SLOTS = 7
SHIFT_SCALE = 2.0
DIAG_CENTER = 4.0
TERMS = 4
SEND_ORDER = (9, 13, 5, 1, 12, 0, 15, 10, 4, 7, 14, 3, 6, 2, 11, 8)
VMEM = pl.BlockSpec(memory_space=pltpu.VMEM)
SMEM = pl.BlockSpec(memory_space=pltpu.SMEM)
ANY = pl.BlockSpec(memory_space=pl.ANY)


def time_filters(length):
    phase = np.exp(-2j * np.pi * np.arange(length) / length)
    step = 1.0 / (DIAG_CENTER + SHIFT_SCALE * (1.0 - phase))
    apart = np.arange(length)[:, None] - np.arange(length)[None, :]
    return [np.fft.ifft(step ** (m + 1)).real[apart % length] for m in range(TERMS)]


def send_order(count):
    return list(SEND_ORDER) if count == len(SEND_ORDER) else list(range(count))


def halves(value):
    high = value.astype(jnp.bfloat16)
    return high, (value - high.astype(jnp.float32)).astype(jnp.bfloat16)


def mm(left, right):
    return jnp.dot(left, right, preferred_element_type=jnp.float32)


def mm_split(left, right_high, right_low):
    rows = left.shape[0]
    high, low = halves(left)
    both = mm(jnp.concatenate([high, low], axis=0), right_high)
    return both[:rows] + both[rows:] + mm(high, right_low)


def filter_mm(table, value):
    rows = table.shape[0] // 2
    high, low = halves(value)
    both = mm(table, high)
    return both[:rows] + both[rows:] + mm(table[:rows], low)


def chosen(even, up_ref, down_ref, index, halo):
    first = jnp.where(even, up_ref[index % halo], down_ref[index % halo])
    second = jnp.where(even, down_ref[index % halo], up_ref[index % halo])
    return first if index < halo else second


def build_kernel(
    count, me_ref, columns_ref, up_ref, down_ref, blocks_in,
    high_ref, low_ref, pick_ref, table_ref, blocks_ref, block_sems,
):
    rows, size, _ = blocks_ref.shape
    halo = up_ref.shape[0]
    pieces = [
        pltpu.make_async_copy(
            blocks_in.at[pl.ds(2 * pair, 2)], blocks_ref.at[pl.ds(2 * pair, 2)], block_sems.at[pair]
        )
        for pair in range(rows // 2)
    ]
    for copy in pieces:
        copy.start()
    me = me_ref[0]
    even = lax.rem(me, 2) == 0
    sent = [chosen(even, up_ref, down_ref, index, halo) for index in range(2 * halo)]
    for index in range(2 * halo):
        table_ref[SLOTS, index] = sent[index]
    for row in range(rows):
        for slot in range(SLOTS):
            column = columns_ref[slot, row]
            if slot in (1, 2):
                column = jnp.where(even, column + (halo if slot == 1 else -halo), column)
            table_ref[slot, row] = column
    lane = lax.broadcasted_iota(jnp.int32, (size, 2 * size), 1)
    inner = lax.broadcasted_iota(jnp.int32, (size, 2 * size), 0)
    for pair in range(rows // 2):
        pieces[pair].wait()
        lanes = slice(pair * 2 * size, (pair + 1) * 2 * size)
        across = -blocks_ref[2 * pair : 2 * pair + 2].reshape(2 * size, SLOTS * size).T
        part = [across[slot * size : (slot + 1) * size] for slot in range(SLOTS)]
        part[0] = part[0] + jnp.where(lax.rem(lane, size) == inner, DIAG_CENTER, 0.0)
        part[1] = jnp.where(me == 0, 0.0, part[1])
        part[2] = jnp.where(me == count - 1, 0.0, part[2])
        for later in range(3, SLOTS):
            for sooner in (0, *range(3, later)):
                same = [columns_ref[later, 2 * pair + half] == columns_ref[sooner, 2 * pair + half] for half in range(2)]
                moved = jnp.where(lane < size, same[0].astype(jnp.int32), same[1].astype(jnp.int32)) > 0
                part[sooner] = part[sooner] + jnp.where(moved, part[later], 0.0)
                part[later] = jnp.where(moved, 0.0, part[later])
        for slot in range(SLOTS):
            high, low = halves(part[slot])
            high_ref[slot * size : (slot + 1) * size, lanes] = high
            low_ref[slot * size : (slot + 1) * size, lanes] = low
    down = lax.broadcasted_iota(jnp.int32, (rows * size, 2 * size), 0)
    across = lax.broadcasted_iota(jnp.int32, (rows * size, 2 * size), 1)
    for pair in range(halo):
        place = jnp.where(across < size, sent[2 * pair], sent[2 * pair + 1] - 1) * size + across
        pick_ref[:, pair * 2 * size : (pair + 1) * 2 * size] = jnp.where(down == place, 1.0, 0.0).astype(jnp.bfloat16)


def store_sent(value, inner_ref, outer_ref):
    width = inner_ref.shape[1]
    inner_ref[...] = value[:, :width]
    outer_ref[...] = value[:, width:]


def picked(value, pick_ref):
    high, low = halves(value)
    rows = high.shape[0]
    both = mm(jnp.concatenate([high, low], axis=0), pick_ref[...])
    return both[:rows] + both[rows:]


def first_kernel(value_ref, pick_ref, inner_ref, outer_ref):
    store_sent(picked(value_ref[...], pick_ref), inner_ref, outer_ref)


def own_first_kernel(
    value_ref, blocks_high, blocks_low, pick_ref, table_in,
    out_ref, sent_ref, high_ref, low_ref, halo_high, halo_low, table_ref, sem,
):
    times, own = value_ref.shape
    size = BS
    rows = own // size
    copy = pltpu.make_async_copy(table_in, table_ref, sem)
    copy.start()
    for ref in (high_ref, low_ref, halo_high, halo_low):
        ref[...] = jnp.zeros_like(ref)
    copy.wait()
    for slot in reversed(range(SLOTS)):
        for row in range(rows):
            at = pl.ds(pl.multiple_of(table_ref[slot, row] * size, size), size)
            lanes = slice(row * size, (row + 1) * size)
            high_ref[at, lanes] = blocks_high[slot * size : (slot + 1) * size, lanes]
            low_ref[at, lanes] = blocks_low[slot * size : (slot + 1) * size, lanes]
    for index in range(sent_ref.shape[1] // size):
        row = table_ref[SLOTS, index]
        half = index % 2
        pair = pl.ds(pl.multiple_of((row // 2) * 2 * size, 2 * size), 2 * size)
        for slot in (1, 2):
            at = pl.ds(pl.multiple_of((table_ref[slot, row] - rows) * size, size), size)
            for whole_ref, few_ref in ((blocks_high, halo_high), (blocks_low, halo_low)):
                tile = whole_ref[slot * size : (slot + 1) * size, pair].astype(jnp.float32)
                tile = jnp.where(lax.rem(row, 2) == half, tile, pltpu.roll(tile, size, 1)).astype(jnp.bfloat16)
                few_ref[at, index * size : (index + 1) * size] = tile[:, half * size : (half + 1) * size]
    out_ref[...] = mm_split(value_ref[...], high_ref[:own], low_ref[:own])
    sent_ref[...] = picked(out_ref[...], pick_ref)


def halo_once(inner_ref, outer_ref, high):
    both = jnp.concatenate([inner_ref[...], outer_ref[...]], axis=1)
    return mm(both.astype(jnp.bfloat16), high)


def halo_product(inner_ref, outer_ref, high, low):
    both = jnp.concatenate([inner_ref[...], outer_ref[...]], axis=1)
    return mm_split(both, high, low)


def send_kernel(part_ref, from_inner, from_outer, halo_high, halo_low, inner_ref, outer_ref):
    value = part_ref[...] + halo_product(from_inner, from_outer, halo_high[...], halo_low[...])
    store_sent(value, inner_ref, outer_ref)


def send_last_kernel(part_ref, from_inner, from_outer, halo_high, table_ref, inner_ref, outer_ref):
    value = part_ref[...] + halo_once(from_inner, from_outer, halo_high[...])
    table = table_ref[: value.shape[0]]
    store_sent(mm(table, value.astype(jnp.bfloat16)), inner_ref, outer_ref)


def own_second_kernel(
    start_ref, part_ref, from_inner, from_outer, high_ref, low_ref, pick_ref, table0_ref, table1_ref,
    out_ref, sent_ref, total_ref,
):
    own = part_ref.shape[1]
    value = part_ref[...] + halo_product(from_inner, from_outer, high_ref[own:], low_ref[own:])
    out_ref[...] = mm_split(value, high_ref[:own], low_ref[:own])
    sent_ref[...] = picked(out_ref[...], pick_ref)
    total_ref[...] = filter_mm(table0_ref[...], start_ref[...]) + filter_mm(table1_ref[...], value)


def own_third_kernel(part_ref, from_inner, from_outer, total_ref, high_ref, low_ref, table2_ref, table3_ref, out_ref):
    own = part_ref.shape[1]
    value = part_ref[...] + halo_product(from_inner, from_outer, high_ref[own:], low_ref[own:])
    filtered = filter_mm(table3_ref[...], value)
    out_ref[...] = (
        total_ref[...] + filter_mm(table2_ref[...], value) + mm_split(filtered, high_ref[:own], low_ref[:own])
    )


def close_kernel(part_ref, from_inner, from_outer, high_ref, out_ref):
    own = part_ref.shape[1]
    out_ref[...] = part_ref[...] + halo_once(from_inner, from_outer, high_ref[own:])


def store_kernel(order, value_ref, out_ref, sem):
    step = value_ref.shape[1] // len(order)
    copies = [
        pltpu.make_async_copy(
            value_ref.at[:, index * step : (index + 1) * step],
            out_ref.at[:, sender * step : (sender + 1) * step],
            sem,
        )
        for index, sender in enumerate(order)
    ]
    for copy in copies:
        copy.start()
    pltpu.make_async_copy(value_ref, out_ref, sem).wait()


def call(kernel, outs, name, ins, out_specs=None, scratch=(), moved=4 << 20):
    return pl.pallas_call(
        kernel,
        out_shape=outs,
        in_specs=ins,
        out_specs=jax.tree.map(lambda _: VMEM, outs) if out_specs is None else out_specs,
        scratch_shapes=scratch,
        name=name,
        compiler_params=pltpu.CompilerParams(vmem_limit_bytes=32 << 20),
        cost_estimate=pl.CostEstimate(flops=1 << 28, bytes_accessed=moved, transcendentals=0),
    )


def per_device(source, blocks, columns, rows_up, rows_down):
    count = lax.axis_size("space")
    rows, halo = blocks.shape[0], rows_up.shape[0]
    own, width = rows * BS, halo * BS
    times = source.shape[0] * count
    me = lax.axis_index("space").reshape(1)
    f32 = lambda *shape: jax.ShapeDtypeStruct(shape, jnp.float32)
    bf16 = lambda *shape: jax.ShapeDtypeStruct(shape, jnp.bfloat16)
    order = send_order(count)
    told = np.arange(times).reshape(count, -1)[np.array(order)].reshape(-1)
    tables = [
        jnp.concatenate(halves(jnp.asarray(table[told], jnp.float32)), axis=0) for table in time_filters(times)
    ]
    inner_pairs = [(i, i ^ 1) for i in range(count)]
    groups = lax.axis_size("group")
    outer_pairs = [
        (group * count + i, group * count + j)
        for group in range(groups)
        for pair in range(1, count - 1, 2)
        for i, j in ((pair, pair + 1), (pair + 1, pair))
    ]
    if groups % 2 == 0:
        outer_pairs += [(group * count + i, (group ^ 1) * count + i) for group in range(groups) for i in (0, count - 1)]

    def swap(inner, outer):
        return lax.ppermute(inner, "space", inner_pairs), lax.ppermute(outer, ("group", "space"), outer_pairs)

    start = lax.all_to_all(source, "space", split_axis=1, concat_axis=0, tiled=True)
    side = own + 2 * width
    dma = pltpu.SemaphoreType.DMA
    *blocked, pick, table = call(
        functools.partial(build_kernel, count),
        (
            *[bf16(SLOTS * BS, own)] * 2,
            bf16(own, 2 * width),
            jax.ShapeDtypeStruct((SLOTS + 1, rows), jnp.int32),
        ),
        "operator",
        [SMEM] * 4 + [ANY],
        (VMEM,) * 3 + (SMEM,),
        scratch=[pltpu.VMEM(blocks.shape, jnp.float32), dma((rows // 2,))],
        moved=16 << 20,
    )(me, columns.T, rows_up, rows_down, blocks)
    sent = (f32(times, width), f32(times, width))
    value, ahead = f32(times, own), f32(times, 2 * width)

    inner, outer = call(first_kernel, sent, "send_0", [VMEM] * 2)(start, pick)
    inner, outer = swap(inner, outer)
    part, part_sent, high, low, *halo_parts = call(
        own_first_kernel,
        (value, ahead, *[bf16(side, own)] * 2, *[bf16(2 * width, 2 * width)] * 2),
        "own_1",
        [VMEM] * 4 + [ANY],
        scratch=[pltpu.SMEM((SLOTS + 1, rows), jnp.int32), dma],
    )(start, *blocked, pick, table)
    next_inner, next_outer = call(send_kernel, sent, "send_1", [VMEM] * 5)(part_sent, inner, outer, *halo_parts)
    next_inner, next_outer = swap(next_inner, next_outer)
    part, part_sent, total = call(own_second_kernel, (value, ahead, value), "own_2", [VMEM] * 9)(
        start, part, inner, outer, high, low, pick, tables[0], tables[1]
    )
    inner, outer = next_inner, next_outer
    next_inner, next_outer = call(send_last_kernel, sent, "send_2", [VMEM] * 5)(
        part_sent, inner, outer, halo_parts[0], tables[3]
    )
    next_inner, next_outer = swap(next_inner, next_outer)
    part = call(own_third_kernel, value, "own_3", [VMEM] * 8)(part, inner, outer, total, high, low, tables[2], tables[3])
    timed = call(close_kernel, value, "close", [VMEM] * 4)(part, next_inner, next_outer, high)
    field = lax.all_to_all(
        timed, "space", split_axis=0, concat_axis=1, tiled=True, axis_index_groups=[order]
    )
    return call(
        functools.partial(store_kernel, order),
        jax.ShapeDtypeStruct(field.shape, field.dtype),
        "store",
        [VMEM],
        ANY,
        scratch=[pltpu.SemaphoreType.DMA],
    )(field)


def solution(mesh):
    placed = (
        P("space", "group"),
        P(("group", "space"), None, None),
        P(("group", "space"), None),
        P(("group", "space")),
        P(("group", "space")),
    )
    return jax.shard_map(
        per_device, mesh=mesh, in_specs=placed, out_specs=P("space", "group"), check_vma=False
    )
```
